32 devices in a mesh: rows: 8 (over y, x, core), cols: 4 (over z).
Axes of the slice: x: 2, y: 2, z: 4, core: 2. Of those that a mesh axis runs over, the one named last changes fastest.
Arguments:
- features: bfloat16 [1, 128, 96, 512], P(None, 'rows', 'cols'), may hold values from -6 to 6
- kernels: bfloat16 [2, 3, 3, 512, 512], replicated, may hold values from -0.09375 to 0.09375
- gains: float32 [2, 512], replicated, may hold values from 0.6 to 1.6
- shifts: float32 [2, 512], replicated, may hold values from -2 to 2
- head_weight: bfloat16 [512, 1792], replicated, may hold values from -0.25 to 0.25
- head_bias: float32 [1792], replicated, may hold values from -2 to 2
- head_scale: float32 [3, 1792], replicated, may hold values from 4 to 16
- scale_id: int32 [1, 16, 12], P(None, 'rows', 'cols'), may hold values from 0 to 2
- valid: int32 [1, 16, 12], P(None, 'rows', 'cols'), may hold values 0 or 1
- cotangent: bfloat16 [1, 128, 96, 1792], P(None, 'rows', 'cols'), may hold values from -6 to 6
Outputs:
- head_out: bfloat16 [1, 128, 96, 1792], P(None, 'rows', 'cols')
- grad_features: float32 [1, 128, 96, 512], P(None, 'rows', 'cols')
- grad_kernels: float32 [2, 3, 3, 512, 512], P(None, None, None, 'rows', 'cols')
- grad_head_weight: float32 [512, 1792], P('rows', 'cols')
- grad_head_bias: float32 [1792], replicated
- grad_head_scale: float32 [3, 1792], replicated
The draws below stay inside these ranges and needn't reach their ends.
All inputs are finite; a program needn't handle non-finite values. No bound on the sum of `valid` on one device may be relied on, other than what follows from the above.
Results may differ from the reference program's by a relative error of at most 0.028.
The reference program's roundings to bfloat16 on the way count: a program that leaves them out, or rounds other values in their place, can miss the bound.
Values may be sent and summed in bfloat16 or wider, within the bound.
No kernel may reach another device: no remote copies, remote signals or barrier semaphores. Data moves between devices by JAX's collectives and lax.ppermute only.
A program may use at most 128 MiB of HBM per device.

```python
import math
import jax
import jax.numpy as jnp
from jax import lax

C = 512
HC = 256
HEADS = 7
SCALES = 3
LAYERS = 2
PBLK = 8
B = 1
H = 128
W = 96
HO = 1792


def with_ends(result, own_key, low, top_value):
    extent = result.shape
    spot = [jax.random.randint(jax.random.fold_in(own_key, axis), (), 0, extent[axis]) for axis in range(len(extent))]
    result = result.at[tuple(spot)].set(low)
    longest = extent.index(max(extent))
    spot[longest] = (spot[longest] + 1) % extent[longest]
    return result.at[tuple(spot)].set(top_value)


def block_scale(rng, dims, pieces, low, largest):
    def one(position, parts):
        steps = jax.random.uniform(jax.random.fold_in(jax.random.fold_in(rng, 6), position), (parts,), jnp.float32, low / len(pieces), largest / len(pieces))
        return jnp.repeat(jnp.exp(steps), dims[position] // parts).reshape((-1,) + (1,) * (len(dims) - position - 1))

    gain = one(*pieces[0])
    for cut in pieces[1:]:
        gain = gain * one(*cut)
    return gain


def gaussian(key, extent, width, reach, split=(), held_as=jnp.bfloat16):
    drawn = jax.random.normal(key, extent, jnp.float32) * width
    if len(split) > 0:
        drawn = block_scale(key, extent, split, -0.22, 0.18) * drawn
    return jnp.clip(drawn, min=-reach, max=reach).astype(held_as)


def setup_inputs(seed: int = 0) -> dict:
    splits = jax.random.split(jax.random.key(seed), 11)
    features = gaussian(splits[0], (B, H, W, C), 1.0, 6.0, ((1, 8), (2, 4)))
    kernels = gaussian(splits[1], (LAYERS, 3, 3, C, C), (9 * C) ** -0.5, 0.09375)
    gains = jnp.clip(jax.random.uniform(splits[2], (LAYERS, C), jnp.float32, 0.6, 1.6), 0.6, 1.6)
    shifts = gaussian(splits[3], (LAYERS, C), 0.3, 2.0, (), jnp.float32)
    head_weight = gaussian(splits[4], (C, HO), C ** -0.5, 0.25)
    head_bias = gaussian(splits[5], (HO,), 0.3, 2.0, (), jnp.float32)
    head_scale = jnp.clip(jnp.exp(jax.random.uniform(splits[6], (SCALES, HO), jnp.float32, math.log(4.0), math.log(16.0))), 4.0, 16.0)
    scale_id = with_ends(jax.random.randint(splits[7], (B, H // PBLK, W // PBLK), 0, 3), jax.random.fold_in(splits[7], 1), 0, 2).astype(jnp.int32)
    valid = with_ends((jax.random.randint(splits[8], (B, H // PBLK, W // PBLK), 0, 4) < 3).astype(jnp.int32), jax.random.fold_in(splits[8], 1), 0, 1)
    cotangent = gaussian(splits[9], (B, H, W, HO), 1.0, 6.0, ((1, 8), (2, 4)))
    return dict(features=features, kernels=kernels, gains=gains, shifts=shifts, head_weight=head_weight, head_bias=head_bias, head_scale=head_scale, scale_id=scale_id, valid=valid, cotangent=cotangent)


@jax.custom_vjp
def low(v):
    return lax.optimization_barrier(v.astype(jnp.bfloat16)).astype(jnp.float32)

@jax.custom_vjp
def low_back(v):
    return v

def low_keep(v):
    return (low(v), None)

def low_pass(kept, grad):
    return (grad,)

def back_keep(v):
    return (v, None)

def back_low(kept, grad):
    return (low(grad),)
low.defvjp(low_keep, low_pass)
low_back.defvjp(back_keep, back_low)
EPS = 1e-06

def conv_same(field, kernel):
    return lax.conv_general_dilated(field, kernel, (1, 1), 'SAME', dimension_numbers=('NHWC', 'HWIO', 'NHWC'), precision=lax.Precision.HIGHEST)

def expand(blocks):
    return jnp.repeat(jnp.repeat(blocks, PBLK, axis=1), PBLK, axis=2)

def reference(features, kernels, gains, shifts, head_weight, head_bias, head_scale, scale_id, valid, cotangent):
    onehot = (expand(scale_id)[..., None] == jnp.arange(SCALES, dtype=jnp.int32)).astype(jnp.float32)
    maskf = expand(valid).astype(jnp.float32)[..., None]

    def forward(inputs, kern, weight, bias, scales):
        act = inputs
        for layer in range(LAYERS):
            conv = low_back(conv_same(low(act), kern[layer]))
            act = jnp.maximum(gains[layer] * conv + shifts[layer], 0.0)
        flat = jnp.einsum('bhwc,ck->bhwk', low(act), weight, precision=lax.Precision.HIGHEST)
        flat = low_back(flat + bias)
        grouped = flat.reshape(flat.shape[:3] + (HEADS, HC))
        inv = lax.rsqrt(lax.optimization_barrier(jnp.sum(grouped * grouped, axis=-1, keepdims=True)) + EPS)
        unit = (grouped * inv).reshape(flat.shape)
        per_pixel = jnp.einsum('bhws,sk->bhwk', onehot, scales, precision=lax.Precision.HIGHEST)
        return maskf * per_pixel * unit
    out, pull = jax.vjp(forward, features.astype(jnp.float32), kernels.astype(jnp.float32), head_weight.astype(jnp.float32), head_bias, head_scale)
    grad_x, grad_k, grad_w, grad_b, grad_s = pull(cotangent.astype(jnp.float32))
    return (out.astype(jnp.bfloat16), grad_x, grad_k, grad_w, grad_b, grad_s)
```

```python
import functools

import jax
import jax.numpy as jnp
from jax import lax
from jax.experimental import pallas as pl
from jax.experimental.pallas import tpu as pltpu
from jax.sharding import PartitionSpec as P

HC = 256
HEADS = 7
SCALES = 3
PBLK = 8
EPS = 1e-06

FH = 4
TH = 2
TAIL = 8

BF = jnp.bfloat16
F32 = jnp.float32
VMEM = pl.BlockSpec(memory_space=pltpu.VMEM)
SMEM = pl.BlockSpec(memory_space=pltpu.SMEM)
ANY = pl.BlockSpec(memory_space=pl.ANY)


def params():
    return pltpu.CompilerParams(vmem_limit_bytes=56 * 1024 * 1024)


def cost(flops, moved):
    return pl.CostEstimate(flops=int(flops), bytes_accessed=int(moved), transcendentals=0)


def nbytes(*arrays):
    return sum(a.size * a.dtype.itemsize for a in arrays)


def in_image(pos_ref, first, count, slot, fw, fh):
    index = lax.broadcasted_iota(jnp.int32, (count, 1), 0)
    place = lax.rem(index, slot)
    ahead = place >= fw + TAIL // 2
    row = pos_ref[0] + lax.div(index, slot) + (first - FH - 1) + jnp.where(ahead, 1, 0)
    col = pos_ref[1] + jnp.where(ahead, place - slot, place)
    inside = (row >= 0) & (row < pos_ref[2]) & (col >= 0) & (col < pos_ref[3])
    return inside.astype(F32)


def fetch(src_ref, dst_ref, sem, order):
    copies = []
    for n, k in enumerate(order):
        copies.append(pltpu.make_async_copy(src_ref.at[k], dst_ref.at[k], sem.at[n]))
    for copy in copies:
        copy.start()
    return copies


ORDER = [3 * i + j for j in (1, 0, 2) for i in range(3)]


def conv(load, copies, w_ref, acc_ref, count, slot, back):
    done = 0
    for n, j in enumerate((1, 0, 2)):
        total = None
        for i in range(3):
            copies[done].wait()
            done += 1
            weight = w_ref[3 * i + j]
            if back:
                term = lax.dot_general(
                    load(2 - i), weight, (((1,), (1,)), ((), ())), preferred_element_type=F32
                )
            else:
                term = jnp.dot(load(i), weight, preferred_element_type=F32)
            total = term if total is None else total + term
        if j == 1:
            acc_ref[...] = total
        else:
            step = 1 if (j == 0) != back else count - 1
            acc_ref[...] += pltpu.roll(total, step, 0)


def forward_kernel(
    fw, fh, pos, core, up, down, tail, kern, gain, shift, act, own, other, x_ref, w_ref, acc_ref, sem
):
    slot = fw + TAIL
    count = act.shape[0]
    copies = fetch(kern, w_ref, sem, ORDER)
    for s in range(fh + 2 * FH + 1):
        at = s * slot
        if s == 0:
            x_ref[at : at + fw] = jnp.zeros((fw, x_ref.shape[1]), BF)
        elif s <= FH:
            x_ref[at : at + fw] = up[s - 1]
        elif s <= FH + fh:
            x_ref[at : at + fw] = core[s - 1 - FH]
        else:
            x_ref[at : at + fw] = down[s - 1 - FH - fh]
        x_ref[at + fw : at + slot] = tail[s]
    conv(lambda i: x_ref[i * slot : i * slot + count], copies, w_ref, acc_ref, count, slot, False)
    pre = gain[...] * acc_ref[...] + shift[...]
    out = (jnp.maximum(pre, 0.0) * in_image(pos, 1, count, slot, fw, fh)).astype(BF)
    act[...] = out
    half = out.shape[1] // 2
    start = 2 * slot + slot // 2
    part = out[start : start + own.shape[0]]
    side = pos[4] == 0
    own[...] = jnp.where(side, part[:, :half], part[:, half:])
    other[...] = jnp.where(side, part[:, half:], part[:, :half])


def head_kernel(
    fw, fh, pos, a1, kern, gain, shift, hw_hbm, bias, scale, ct, ct_code, ct_up, ct_down, ct_tail,
    head_out, dy, dy_own, dy_other, keep, send, small,
    w_ref, hw_ref, acc_ref, a2_ref, at_ref, ct_ref, code_ref, part_ref, sem, hw_sem,
):
    slot = fw + TAIL
    count = dy.shape[0]
    copies = fetch(kern, w_ref, sem, ORDER)
    hw_copy = pltpu.make_async_copy(hw_hbm, hw_ref, hw_sem)
    hw_copy.start()
    conv(lambda i: a1[i * slot : i * slot + count], copies, w_ref, acc_ref, count, slot, False)
    pre = gain[...] * acc_ref[...] + shift[...]
    act = jnp.maximum(pre, 0.0).astype(BF)
    a2_ref[...] = act
    rows = fh + 2 * TH + 1
    ho = ct.shape[2]
    lo, hi = (TH + 1) * slot, (TH + 1 + fh) * slot
    index = lax.broadcasted_iota(jnp.int32, (hi - lo, 1), 0)
    inner = lax.rem(index, slot) < fw
    at_ref[...] = jnp.where(inner, act[lo:hi], jnp.zeros_like(act[lo:hi])).T

    def place(dst, lanes, first):
        dst[0:fw] = jnp.zeros((fw, dst.shape[1]), dst.dtype)
        for s in range(1, rows):
            if s <= TH:
                piece = ct_up[s - 1, :, lanes]
            elif s <= TH + fh:
                piece = first[s - 1 - TH]
            else:
                piece = ct_down[s - 1 - TH - fh, :, lanes]
            dst[s * slot : s * slot + fw] = piece
        for s in range(rows):
            dst[s * slot + fw : (s + 1) * slot] = ct_tail[s, :, lanes]

    place(code_ref, pl.ds(ho, 128), ct_code)
    code = code_ref[:, 0:1].astype(F32)
    lane = lax.broadcasted_iota(jnp.int32, (hi - lo, 128), 1)
    level = jnp.where(lane < SCALES, lane + 1, -1).astype(F32)
    hot = jnp.where(inner & ((code[lo:hi] == level) | (lane == SCALES)), 1.0, 0.0).astype(BF).T[:16]
    acc_ref[...] = jnp.zeros_like(acc_ref)
    hw_copy.wait()
    chip = pos[6]
    core = pos[7]

    def one(g, carry):
        lanes = pl.ds(pl.multiple_of(g * HC, HC), HC)
        place(ct_ref, lanes, ct.at[:, :, lanes])
        weight = hw_ref[:, lanes]
        h = jnp.dot(a2_ref[...], weight, preferred_element_type=F32) + bias[:, lanes]
        inv = lax.rsqrt(jnp.sum(h * h, axis=1, keepdims=True) + EPS)
        u = h * inv
        s = jnp.where(code == 1.0, scale[0:1, lanes], 0.0)
        for k in range(1, SCALES):
            s = jnp.where(code == k + 1.0, scale[k : k + 1, lanes], s)
        out = (s * u)[lo:hi].astype(BF)
        for r in range(fh):
            head_out[r, :, lanes] = out[r * slot : r * slot + fw]
        up = ct_ref[...].astype(F32)
        du = up * s
        along = jnp.sum(du * u, axis=1, keepdims=True)
        dh = (inv * (du - u * along)).astype(BF)
        acc_ref[...] += lax.dot_general(
            dh, weight, (((1,), (1,)), ((), ())), preferred_element_type=F32
        )
        dh_core = dh[lo:hi]
        part_ref[...] = jnp.dot(at_ref[...], dh_core, preferred_element_type=F32)
        gu = (up * u)[lo:hi].astype(BF)
        scale_part = jnp.dot(hot, gu, preferred_element_type=F32)
        bias_part = jnp.dot(hot, dh_core, preferred_element_type=F32)
        pick = lax.broadcasted_iota(jnp.int32, scale_part.shape, 0)
        small[:, lanes] = jnp.where(pick < SCALES, scale_part, bias_part)
        size = keep.shape[1]
        for m in range(keep.shape[0]):
            block = 2 * lax.bitwise_xor(chip, m)
            mine = pl.multiple_of((block + core) * size, size)
            theirs = pl.multiple_of((block + 1 - core) * size, size)
            keep[m, :, lanes] = part_ref[pl.ds(mine, size), :].astype(BF)
            send[m, :, lanes] = part_ref[pl.ds(theirs, size), :].astype(BF)
        return carry

    lax.fori_loop(0, HEADS, one, 0)
    grad = jnp.where(a2_ref[...] > 0.0, gain[...] * acc_ref[...], 0.0).astype(BF)
    dy[...] = grad
    half = grad.shape[1] // 2
    side = pos[5] == 0
    for r in range(fh):
        at = lo + r * slot
        left, right = grad[at : at + fw, :half], grad[at : at + fw, half:]
        dy_own[r] = jnp.where(side, left, right)
        dy_other[r] = jnp.where(side, right, left)


def back_kernel(fw, fh, pos, dy2, kern, gain, a1, dy1, own, other, w_ref, acc_ref, sem):
    slot = fw + TAIL
    count = dy1.shape[0]
    copies = fetch(kern, w_ref, sem, ORDER)
    conv(lambda i: dy2[i * slot : i * slot + count], copies, w_ref, acc_ref, count, slot, True)
    grad = jnp.where(
        a1[2 * slot : 2 * slot + count] > 0.0, gain[...] * acc_ref[...], 0.0
    ).astype(BF)
    dy1[...] = grad
    half = grad.shape[1] // 2
    start = slot // 2
    part = grad[start : start + own.shape[0]]
    side = pos[5] == 0
    own[...] = jnp.where(side, part[:, :half], part[:, half:])
    other[...] = jnp.where(side, part[:, half:], part[:, :half])


def input_kernel(fw, fh, dy1, kern, out, w_ref, acc_ref, sem):
    slot = fw + TAIL
    lead = slot // 2
    count = fh * slot + lead
    copies = fetch(kern, w_ref, sem, ORDER)
    conv(
        lambda i: dy1[(i + 1) * slot - lead : (i + 1) * slot - lead + count],
        copies, w_ref, acc_ref, count, slot, True,
    )
    for r in range(fh):
        out[r] = acc_ref[lead + r * slot : lead + r * slot + fw]


def weight_kernel(fw, fh, forward, pos, *refs):
    slot = fw + TAIL
    flat, wide = refs[0:4], refs[4:8]
    keep, send, turn_ref, shift_ref = refs[8:]
    core = pos[7]
    full = fh * slot
    length = wide[0].shape[0]
    lanes = wide[0].shape[1]
    for b in range(4):
        rows = []
        gap = jnp.zeros((TAIL, lanes), BF)
        for r in range(fh):
            rows += [flat[b][r], gap]
        turn_ref[:, b * full : (b + 1) * full] = jnp.concatenate(rows, axis=0).T
        value = wide[b][...]
        wider = value.astype(F32)
        shift_ref[0, b] = pltpu.roll(wider, 1, 0).astype(BF)
        shift_ref[1, b] = value
        shift_ref[2, b] = pltpu.roll(wider, length - 1, 0).astype(BF)
    base = slot + slot // 2
    size = keep.shape[2]
    part = keep.shape[3]
    for i in range(3):
        for j in range(3):
            row, col = (i, j) if forward else (2 - i, 2 - j)
            at = base + (row - 1) * slot
            total = None
            for b in range(4):
                term = jnp.dot(
                    turn_ref[:, b * full : (b + 1) * full],
                    shift_ref[col, b, at : at + full],
                    preferred_element_type=F32,
                )
                total = term if total is None else total + term
            if forward:
                total = total.T
            total = total.astype(BF)
            left, right = total[:, :part], total[:, part:]
            mine = jnp.where(core == 0, left, right)
            theirs = jnp.where(core == 0, right, left)
            for z in range(keep.shape[0]):
                keep[z, 3 * i + j] = mine[z * size : (z + 1) * size]
                send[z, 3 * i + j] = theirs[z * size : (z + 1) * size]


def shifted(array, axis, step):
    peers = lax.axis_size(axis)
    pairs = [(i, i + step) for i in range(peers) if 0 <= i + step < peers]
    return lax.ppermute(array, axis, pairs)


def crossed(array, bits):
    peers = lax.axis_size("rows")
    return lax.ppermute(array, "rows", [(i, i ^ bits) for i in range(peers)])


def rim_tail(left, right):
    half = TAIL // 2
    wide = left.shape[1]
    left = jnp.pad(left, ((0, 1), (half - wide, 0), (0, 0)))
    right = jnp.pad(right, ((1, 0), (0, half - wide), (0, 0)))
    return jnp.concatenate([right, left], axis=1)


def shards(
    features, kernels, gains, shifts, head_weight, head_bias, head_scale, scale_id, valid, cotangent
):
    rows, cols = lax.axis_size("rows"), lax.axis_size("cols")
    row, col = lax.axis_index("rows"), lax.axis_index("cols")
    feat, ct = features[0], cotangent[0]
    fh, fw, ch = feat.shape
    ho = ct.shape[2]
    slot = fw + TAIL
    core, xbit, ybit = row & 1, (row >> 1) & 1, (row >> 2) & 1
    pos = jnp.stack(
        [row * fh, col * fw, jnp.full_like(row, rows * fh), jnp.full_like(row, cols * fw)]
        + [xbit, ybit, (row >> 1) & 3, core]
    ).astype(jnp.int32)
    taps = kernels.reshape(2, 9, ch, ch)

    f_up, f_down = shifted(feat[-FH:], "rows", 1), shifted(feat[:FH], "rows", -1)
    blocks = jnp.where(valid[0] == 1, scale_id[0] + 1, 0).astype(BF)
    code = jnp.repeat(jnp.repeat(blocks, PBLK, axis=0), PBLK, axis=1)
    code = jnp.broadcast_to(code[:, :, None], (fh, fw, 128))
    top = jnp.concatenate([ct[:TH], code[:TH]], axis=2)
    bottom = jnp.concatenate([ct[-TH:], code[-TH:]], axis=2)
    c_up, c_down = shifted(bottom, "rows", 1), shifted(top, "rows", -1)
    edges = [jnp.concatenate([f_up[:, e], feat[:, e], f_down[:, e]], axis=0) for e in (slice(0, FH), slice(-FH, None))]
    f_left, f_right = shifted(edges[1], "cols", 1), shifted(edges[0], "cols", -1)
    f_tail = rim_tail(f_left, f_right)
    edges = []
    for e in (slice(0, TH), slice(-TH, None)):
        middle = jnp.concatenate([ct[:, e], code[:, e]], axis=2)
        edges.append(jnp.concatenate([c_up[:, e], middle, c_down[:, e]], axis=0))
    c_left, c_right = shifted(edges[1], "cols", 1), shifted(edges[0], "cols", -1)
    c_tail = rim_tail(c_left, c_right)

    w_scratch = pltpu.VMEM((9, ch, ch), BF)
    w_sem = pltpu.SemaphoreType.DMA((9,))
    flop = 2 * ch * ch * 9
    n1 = (fh + 2 * FH - 1) * slot
    wide = (fh + 2) * slot + slot // 2
    half = ch // 2
    shape = jax.ShapeDtypeStruct
    a1, a1_own, a1_other = pl.pallas_call(
        functools.partial(forward_kernel, fw, fh),
        out_shape=(shape((n1, ch), BF), shape((wide, half), BF), shape((wide, half), BF)),
        in_specs=[SMEM, VMEM, VMEM, VMEM, VMEM, ANY, VMEM, VMEM],
        out_specs=(VMEM,) * 3,
        scratch_shapes=[
            pltpu.VMEM(((fh + 2 * FH + 1) * slot, ch), BF),
            w_scratch,
            pltpu.VMEM((n1, ch), F32),
            w_sem,
        ],
        compiler_params=params(),
        cost_estimate=cost(n1 * flop, 9 * ch * ch * 2),
        name="conv1",
    )(pos, feat, f_up, f_down, f_tail, taps[0], gains[0:1], shifts[0:1])

    n2 = (fh + 2 * TH + 1) * slot
    span = fh * slot
    size = ch // 8
    head_out, dy2, dy2_own, dy2_other, hw_keep, hw_send, small = pl.pallas_call(
        functools.partial(head_kernel, fw, fh),
        out_shape=(
            shape((fh, fw, ho), BF),
            shape((n2, ch), BF),
            shape((fh, fw, half), BF),
            shape((fh, fw, half), BF),
            shape((4, size, ho), BF),
            shape((4, size, ho), BF),
            shape((16, ho), F32),
        ),
        in_specs=[SMEM, VMEM, ANY, VMEM, VMEM, ANY, VMEM, VMEM] + [VMEM] * 5,
        out_specs=(VMEM,) * 7,
        scratch_shapes=[
            w_scratch,
            pltpu.VMEM((ch, ho), BF),
            pltpu.VMEM((n2, ch), F32),
            pltpu.VMEM((n2, ch), BF),
            pltpu.VMEM((ch, span), BF),
            pltpu.VMEM((n2, HC), BF),
            pltpu.VMEM((n2, 128), BF),
            pltpu.VMEM((ch, HC), F32),
            w_sem,
            pltpu.SemaphoreType.DMA,
        ],
        compiler_params=params(),
        cost_estimate=cost(n2 * (flop + 4 * ch * ho) + 2 * span * ch * ho, 9 * ch * ch * 2),
        name="head",
    )(
        pos, a1, taps[1], gains[1:2], shifts[1:2], head_weight, head_bias[None], head_scale,
        ct, code, c_up, c_down, c_tail,
    )

    n3 = (fh + 3) * slot
    dy1, dy1_own, dy1_other = pl.pallas_call(
        functools.partial(back_kernel, fw, fh),
        out_shape=(shape((n3, ch), BF), shape((wide, half), BF), shape((wide, half), BF)),
        in_specs=[SMEM, VMEM, ANY, VMEM, VMEM],
        out_specs=(VMEM,) * 3,
        scratch_shapes=[w_scratch, pltpu.VMEM((n3, ch), F32), w_sem],
        compiler_params=params(),
        cost_estimate=cost(n3 * flop, 9 * ch * ch * 2),
        name="back2",
    )(pos, dy2, taps[1], gains[0:1], a1)

    grad_features = pl.pallas_call(
        functools.partial(input_kernel, fw, fh),
        out_shape=shape((fh, fw, ch), F32),
        in_specs=[VMEM, ANY],
        out_specs=VMEM,
        scratch_shapes=[w_scratch, pltpu.VMEM((span + slot // 2, ch), F32), w_sem],
        compiler_params=params(),
        cost_estimate=cost(span * flop, 9 * ch * ch * 2),
        name="back1",
    )(dy1, taps[0])

    if rows == 8 and cols == 4:
        halves = feat.reshape(fh, fw, 2, half)
        feat_own = jnp.where(xbit == 0, halves[:, :, 0], halves[:, :, 1])
        feat_other = jnp.where(xbit == 0, halves[:, :, 1], halves[:, :, 0])
        feats = [feat_own, crossed(feat_other, 2), crossed(feat_own, 4), crossed(feat_other, 6)]
        a1s = [a1_own, crossed(a1_other, 2), crossed(a1_own, 4), crossed(a1_other, 6)]
        dy2s = [dy2_own, crossed(dy2_own, 2), crossed(dy2_other, 4), crossed(dy2_other, 6)]
        dy1s = [dy1_own, crossed(dy1_own, 2), crossed(dy1_other, 4), crossed(dy1_other, 6)]

        def kernel_part(flat, wider, forward, name):
            keep, send = pl.pallas_call(
                functools.partial(weight_kernel, fw, fh, forward),
                out_shape=(shape((4, 9, half // 4, half // 2), BF),) * 2,
                in_specs=[SMEM] + [VMEM] * 8,
                out_specs=(VMEM,) * 2,
                scratch_shapes=[pltpu.VMEM((half, 4 * span), BF), pltpu.VMEM((3, 4, wide, half), BF)],
                compiler_params=params(),
                cost_estimate=cost(span * flop, 4 * nbytes(*flat, *wider)),
                name=name,
            )(pos, *flat, *wider)
            total = keep + crossed(send, 1)
            mine = lax.psum_scatter(total, "cols", scatter_dimension=0, tiled=True)[0]
            pairs = []
            for r in range(8):
                for c in range(4):
                    to_row = 4 * ((r >> 1) & 1) + c
                    to_col = 2 * (r >> 2) + (r & 1)
                    pairs.append((4 * r + c, 4 * to_row + to_col))
            return lax.ppermute(mine, ("rows", "cols"), pairs)

        part2 = kernel_part(dy2s, a1s, True, "grad2")
        part1 = kernel_part(feats, dy1s, False, "grad1")
        grad_kernels = jnp.stack([part1, part2]).astype(F32).reshape(2, 3, 3, half // 4, half // 2)

        pair = hw_keep.astype(F32) + crossed(hw_send, 1).astype(F32)
        pair = pair.astype(BF)
        parts = [pair[0]] + [crossed(pair[m], 2 * m) for m in (1, 2, 3)]
        mine = sum(p.astype(F32) for p in parts).astype(BF)
        grad_head_weight = lax.psum_scatter(mine, "cols", scatter_dimension=1, tiled=True).astype(F32)

        small = small[:4]
        for bits in (1, 2, 4):
            small = small + crossed(small, bits)
        for bits in (1, 2):
            small = small + lax.ppermute(small, "cols", [(i, i ^ bits) for i in range(cols)])
        grad_head_scale, grad_head_bias = small[:SCALES], small[SCALES]
    else:
        flat = jnp.pad(feat, ((0, 0), (0, TAIL), (0, 0))).reshape(span, ch)
        dy2_flat = dy2[(TH + 1) * slot :][:span].reshape(fh, slot, ch)[:, :fw]
        dy2_flat = jnp.pad(dy2_flat, ((0, 0), (0, TAIL), (0, 0))).reshape(span, ch)
        parts = []
        for left, right, first, sign in ((flat, jnp.pad(dy1, ((0, 8), (0, 0))), 2, -1), (a1, dy2_flat, 4, 1)):
            for i in (-1, 0, 1):
                for j in (-1, 0, 1):
                    at = (first + sign * i) * slot + sign * j
                    if sign < 0:
                        pair = (left, right[at : at + span])
                    else:
                        pair = (left[at : at + span], right)
                    parts.append(jnp.einsum("pc,pk->ck", *pair, preferred_element_type=F32).astype(BF))
        total = jnp.stack(parts).reshape(2, 3, 3, ch, ch)
        total = lax.psum_scatter(total, "cols", scatter_dimension=4, tiled=True)
        grad_kernels = lax.psum_scatter(
            total.astype(F32), "rows", scatter_dimension=3, tiled=True
        )
        at = (row >> 1) & 3
        order = [(at ^ m) * 2 for m in range(4)]
        blocks = jnp.zeros((8, size, ho), BF)
        for m in range(4):
            blocks = lax.dynamic_update_slice(blocks, hw_keep[m : m + 1], (order[m] + core, 0, 0))
            blocks = lax.dynamic_update_slice(blocks, hw_send[m : m + 1], (order[m] + 1 - core, 0, 0))
        part = lax.psum_scatter(blocks.reshape(ch, ho), "cols", scatter_dimension=1, tiled=True)
        grad_head_weight = lax.psum_scatter(part.astype(F32), "rows", scatter_dimension=0, tiled=True)
        small = lax.psum(small[:4], ("rows", "cols"))
        grad_head_scale, grad_head_bias = small[:SCALES], small[SCALES]
    return (
        head_out[None],
        grad_features[None],
        grad_kernels,
        grad_head_weight,
        grad_head_bias,
        grad_head_scale,
    )


def solution(mesh):
    return jax.shard_map(
        shards,
        mesh=mesh,
        in_specs=(
            P(None, "rows", "cols", None),
            P(),
            P(),
            P(),
            P(),
            P(),
            P(),
            P(None, "rows", "cols"),
            P(None, "rows", "cols"),
            P(None, "rows", "cols", None),
        ),
        out_specs=(
            P(None, "rows", "cols", None),
            P(None, "rows", "cols", None),
            P(None, None, None, "rows", "cols"),
            P("rows", "cols"),
            P(),
            P(),
        ),
        check_vma=False,
    )
```

```python
import functools

import jax
import jax.numpy as jnp
from jax import lax
from jax.experimental import pallas as pl
from jax.experimental.pallas import tpu as pltpu
from jax.sharding import PartitionSpec as P

HC = 256
HEADS = 7
SCALES = 3
PBLK = 8
EPS = 1e-06

FH = 4
TH = 2
TAIL = 8

BF = jnp.bfloat16
F32 = jnp.float32
VMEM = pl.BlockSpec(memory_space=pltpu.VMEM)
HBM = pl.BlockSpec(memory_space=pltpu.HBM)
SMEM = pl.BlockSpec(memory_space=pltpu.SMEM)
DMA = pltpu.SemaphoreType.DMA


def place():
    row, col = lax.axis_index("rows"), lax.axis_index("cols")
    return row, col, row & 1, (row >> 1) & 1, (row >> 2) & 1, (row >> 1) & 3


def in_image(first, count, slot, fw, fh):
    index = lax.broadcasted_iota(jnp.int32, (count, 1), 0)
    spot = lax.rem(index, slot)
    ahead = spot >= fw + TAIL // 2
    at_row, at_col = place()[:2]
    row = at_row * fh + lax.div(index, slot) + (first - FH - 1) + jnp.where(ahead, 1, 0)
    col = at_col * fw + jnp.where(ahead, spot - slot, spot)
    high, wide = lax.axis_size("rows") * fh, lax.axis_size("cols") * fw
    inside = (row >= 0) & (row < high) & (col >= 0) & (col < wide)
    return inside.astype(F32)


def conv(load, w_ref, acc_ref, count, back):
    for j in (1, 0, 2):
        total = None
        for i in range(3):
            weight = w_ref[3 * i + j]
            if back:
                term = lax.dot_general(
                    load(2 - i), weight, (((1,), (1,)), ((), ())), preferred_element_type=F32
                )
            else:
                term = jnp.dot(load(i), weight, preferred_element_type=F32)
            total = term if total is None else total + term
        if j == 1:
            acc_ref[...] = total
        else:
            step = 1 if (j == 0) != back else count - 1
            acc_ref[...] += pltpu.roll(total, step, 0)


def rimmed(src_ref, first, slot, fw, fh, side, own, other):
    half = own.shape[2]
    for r in range(fh + 4):
        if r < fh + 2:
            part = src_ref[first + r * slot : first + r * slot + fw]
        else:
            at = first - 1 if r == fh + 2 else first + fw
            part = [src_ref[at + t * slot : at + t * slot + 1] for t in range(fh + 2)]
            part = jnp.concatenate(part + [jnp.zeros((fw - fh - 2, 2 * half), F32)], axis=0)
        part = part.astype(BF)
        own[r] = jnp.where(side, part[:, :half], part[:, half:])
        other[r] = jnp.where(side, part[:, half:], part[:, :half])


def prepare_kernel(
    fw, fh, feat_hbm, ct_hbm, ids, valid,
    feat, ct, code, f_near, f_far, c_near, c_far, edge0, edge1, own, other,
    sems,
):
    moves = ((feat_hbm, feat), (ct_hbm, ct))
    moves = [pltpu.make_async_copy(src, dst, sems.at[n]) for n, (src, dst) in enumerate(moves)]
    for move in moves:
        move.start()
    moves[0].wait()
    ho = ct.shape[2]
    half = own.shape[2]
    row, col, core, xbit, ybit, chip = place()
    for r in range(FH):
        top, bottom = feat[r], feat[fh - FH + r]
        f_near[r] = jnp.where(core == 0, bottom, top)
        f_far[r] = jnp.where(core == 0, top, bottom)
    for r in range(fh):
        low, high = feat[r, :, :half], feat[r, :, half:]
        own[r] = jnp.where(ybit == 0, low, high)
        other[r] = jnp.where(ybit == 0, high, low)
        pieces = []
        for c in range(fw // PBLK):
            at = (r // PBLK, c)
            value = jnp.where(valid[at] == 1, ids[at] + 1, 0)
            pieces.append(jnp.full((PBLK, 128), value.astype(F32), F32))
        code[r] = jnp.concatenate(pieces, axis=0).astype(BF)
    moves[1].wait()
    for r in range(TH):
        for lanes, src in ((slice(0, ho), ct), (slice(ho, ho + 128), code)):
            top, bottom = src[r], src[fh - TH + r]
            c_near[r, :, lanes] = jnp.where(core == 0, bottom, top)
            c_far[r, :, lanes] = jnp.where(core == 0, top, bottom)
    for out, at in ((edge0, 0), (edge1, fw - TH)):
        out[:, :, 0:ho] = ct[:, at : at + TH]
        out[:, :, ho:] = code[:, at : at + TH]


def load_kernel(layer, src_hbm, *refs):
    count = (len(refs) - 1) // 2
    sems = refs[-1]
    extra = refs[: len(refs) // 2 - 1] if len(refs) > 2 else ()
    dst = refs[len(extra)]
    moves = [pltpu.make_async_copy(src_hbm.at[layer], dst, sems.at[0])]
    for n, src in enumerate(extra):
        moves.append(pltpu.make_async_copy(src, refs[len(extra) + 1 + n], sems.at[1 + n]))
    for move in moves:
        move.start()
    for move in moves:
        move.wait()


def lengthen_kernel(reach, bits, core_ref, near, far, out_near, out_far):
    more = near.shape[0]
    fh = out_near.shape[0] - 2 * more
    fw = near.shape[1]
    row, col, core = place()[:3]
    odd = lax.rem(col, 2)
    for r in range(fh + 2 * more):
        edges = []
        for at in (0, fw - reach):
            if r < more:
                edge = jnp.where(core == 0, far[r, at : at + reach], near[r, at : at + reach])
            elif r < more + fh:
                edge = core_ref[r - more, at : at + reach]
            else:
                edge = jnp.where(
                    core == 0, near[r - more - fh, at : at + reach], far[r - more - fh, at : at + reach]
                )
            edges.append(edge)
        out_near[r] = jnp.where(odd == 0, edges[1], edges[0])
        out_far[r] = jnp.where(odd == 0, edges[0], edges[1])


def lengthen_parts_kernel(reach, edge0, edge1, near, far, out_near, out_far):
    more = near.shape[0]
    fh = edge0.shape[0]
    fw = near.shape[1]
    row, col, core = place()[:3]
    odd = lax.rem(col, 2)
    for r in range(fh + 2 * more):
        edges = []
        for edge, at in ((edge0, 0), (edge1, fw - reach)):
            if r < more:
                edge = jnp.where(core == 0, far[r, at : at + reach], near[r, at : at + reach])
            elif r < more + fh:
                edge = edge[r - more]
            else:
                edge = jnp.where(
                    core == 0, near[r - more - fh, at : at + reach], far[r - more - fh, at : at + reach]
                )
            edges.append(edge)
        out_near[r] = jnp.where(odd == 0, edges[1], edges[0])
        out_far[r] = jnp.where(odd == 0, edges[0], edges[1])


def forward_kernel(
    fw, fh, feat, r_near, r_far, c_near, c_far, kern, gains, shifts, act, own, other, x_ref, acc_ref
):
    slot = fw + TAIL
    count = act.shape[0]
    ch = x_ref.shape[1]
    row, col, core, xbit, ybit, chip = place()
    odd = lax.rem(col, 2)
    none = jnp.zeros((FH, ch), BF)
    for s in range(fh + 2 * FH + 1):
        at = s * slot
        if s == 0:
            piece = jnp.zeros((fw, ch), BF)
        elif s <= FH:
            piece = jnp.where(core == 0, r_far[s - 1], r_near[s - 1])
        elif s <= FH + fh:
            piece = feat[s - 1 - FH]
        else:
            piece = jnp.where(core == 0, r_near[s - 1 - FH - fh], r_far[s - 1 - FH - fh])
        x_ref[at : at + fw] = piece
        right = left = none
        if s > 0:
            right = jnp.where(odd == 0, c_near[s - 1], c_far[s - 1])
        if s < fh + 2 * FH:
            left = jnp.where(odd == 0, c_far[s], c_near[s])
        x_ref[at + fw : at + slot] = jnp.concatenate([right, left], axis=0)
    conv(lambda i: x_ref[i * slot : i * slot + count], kern, acc_ref, count, False)
    pre = gains[0:1] * acc_ref[...] + shifts[0:1]
    out = (jnp.maximum(pre, 0.0) * in_image(1, count, slot, fw, fh)).astype(BF)
    act[...] = out
    acc_ref[...] = out.astype(F32)
    rimmed(acc_ref, 3 * slot, slot, fw, fh, ybit == 0, own, other)


def head_kernel(
    fw, fh, a1, kern, gains, shifts, hw_ref, bias, scale, ct, ct_code, r_near, r_far, c_near, c_far,
    head_out, dy, dy_own, dy_other, turned, dh_ref, gu_ref, hot,
    acc_ref, a2_ref, ct_ref, code_ref, h_ref, s_ref, level_ref,
):
    slot = fw + TAIL
    count, ch = dy.shape
    ho = ct.shape[2]
    rows = fh + 2 * TH + 1
    lo, hi = (TH + 1) * slot, (TH + 1 + fh) * slot
    row, col, core, xbit, ybit, chip = place()
    odd = lax.rem(col, 2)

    def spread(dst, lanes, first):
        wide = dst.shape[1]
        dst[0:fw] = jnp.zeros((fw, wide), BF)
        none = jnp.zeros((TH, wide), BF)
        for s in range(rows):
            if 0 < s <= TH:
                dst[s * slot : s * slot + fw] = jnp.where(
                    core == 0, r_far[s - 1, :, lanes], r_near[s - 1, :, lanes]
                )
            elif TH < s <= TH + fh:
                dst[s * slot : s * slot + fw] = first(s - 1 - TH)
            elif s > 0:
                at = s - 1 - TH - fh
                dst[s * slot : s * slot + fw] = jnp.where(
                    core == 0, r_near[at, :, lanes], r_far[at, :, lanes]
                )
            right = left = none
            if s > 0:
                right = jnp.where(odd == 0, c_near[s - 1, :, lanes], c_far[s - 1, :, lanes])
            if s < rows - 1:
                left = jnp.where(odd == 0, c_far[s, :, lanes], c_near[s, :, lanes])
            tail = [right, jnp.zeros((TAIL - 2 * TH, wide), BF), left]
            dst[s * slot + fw : (s + 1) * slot] = jnp.concatenate(tail, axis=0)

    conv(lambda i: a1[i * slot : i * slot + count], kern, acc_ref, count, False)
    act = jnp.maximum(gains[1:2] * acc_ref[...] + shifts[1:2], 0.0).astype(BF)
    a2_ref[...] = act
    index = lax.broadcasted_iota(jnp.int32, (hi - lo, 1), 0)
    inner = lax.rem(index, slot) < fw
    turned[...] = jnp.where(inner, act[lo:hi], jnp.zeros_like(act[lo:hi])).T
    spread(code_ref, pl.ds(ho, 128), lambda r: ct_code[r])
    code = code_ref[...].astype(F32)
    lane = lax.broadcasted_iota(jnp.int32, (count, 128), 1)
    turn = jnp.where(lane < SCALES, lane, jnp.where(lane < 2 * SCALES, lane - SCALES, lane - 2 * SCALES))
    wanted = jnp.where(lane < 3 * SCALES, turn + 1, -1).astype(F32)
    level = jnp.where(code == wanted, 1.0, 0.0)
    level_ref[...] = level.astype(BF)
    core_level = jnp.where(lane[lo:hi] < SCALES, level[lo:hi], jnp.where(lane[lo:hi] == SCALES, 1.0, 0.0))
    hot[...] = jnp.where(inner, core_level, 0.0).astype(BF).T[: hot.shape[0]]

    def product(g):
        lanes = pl.ds(pl.multiple_of(jnp.minimum(g, HEADS - 1) * HC, HC), HC)
        h_ref[lax.rem(g, 2)] = jnp.dot(a2_ref[...], hw_ref[:, lanes], preferred_element_type=F32)

    product(0)
    block = count // rows * 3

    def one(g, carry):
        lanes = pl.ds(pl.multiple_of(g * HC, HC), HC)
        product(g + 1)
        spread(ct_ref, lanes, lambda r: ct[r, :, lanes])
        whole = scale[:, lanes]
        terms = []
        for _ in range(3):
            term = whole.astype(BF)
            terms.append(term.astype(F32))
            whole = whole - terms[-1]
        terms.append(jnp.zeros((128 - 3 * SCALES, HC), F32))
        terms = jnp.concatenate(terms, axis=0).astype(BF)
        s_ref[...] = jnp.dot(level_ref[...], terms, preferred_element_type=F32)
        offset = bias[lanes]
        for at in range(0, count, block):
            here = slice(at, at + block)
            h = h_ref[lax.rem(g, 2), here] + offset
            inv = lax.rsqrt(jnp.sum(h * h, axis=1, keepdims=True) + EPS)
            u = h * inv
            s = s_ref[here]
            up = ct_ref[here].astype(F32)
            du = up * s
            along = jnp.sum(du * u, axis=1, keepdims=True)
            dh_ref[here, lanes] = (inv * (du - u * along)).astype(BF)
            gu_ref[here, lanes] = (up * u).astype(BF)
            out = (s * u).astype(BF)
            for r in range(at // slot, (at + block) // slot):
                if TH + 1 <= r < TH + 1 + fh:
                    head_out[r - TH - 1, :, lanes] = out[r * slot - at : r * slot - at + fw]
        return carry

    lax.fori_loop(0, HEADS, one, 0)
    acc_ref[...] = lax.dot_general(
        dh_ref[...], hw_ref[...], (((1,), (1,)), ((), ())), preferred_element_type=F32
    )
    grad = jnp.where(a2_ref[...] > 0.0, gains[1:2] * acc_ref[...], 0.0).astype(BF)
    dy[...] = grad
    half = ch // 2
    for r in range(fh):
        at = lo + r * slot
        left, right = grad[at : at + fw, :half], grad[at : at + fw, half:]
        dy_own[r] = jnp.where(xbit == 0, left, right)
        dy_other[r] = jnp.where(xbit == 0, right, left)


def head_weight_kernel(lo, turned, dh_ref, gu_ref, hot, keep, send, small, part_ref):
    size = keep.shape[0] // 4
    span = turned.shape[1]
    row, col, core, xbit, ybit, chip = place()

    def one(g, carry):
        lanes = pl.ds(pl.multiple_of(g * HC, HC), HC)
        dh = dh_ref[lo : lo + span, lanes]
        part_ref[...] = jnp.dot(turned[...], dh, preferred_element_type=F32)
        scale_part = jnp.dot(hot[...], gu_ref[lo : lo + span, lanes], preferred_element_type=F32)
        bias_part = jnp.dot(hot[...], dh, preferred_element_type=F32)
        pick = lax.broadcasted_iota(jnp.int32, scale_part.shape, 0)
        rest = jnp.where(pick < SCALES, scale_part, bias_part)
        small[:, lanes] = rest
        for m in range(4):
            block = 2 * lax.bitwise_xor(chip, m)
            mine = pl.multiple_of((block + core) * size, size)
            theirs = pl.multiple_of((block + 1 - core) * size, size)
            keep[m * size : (m + 1) * size, lanes] = part_ref[pl.ds(mine, size), :].astype(BF)
            send[m * size : (m + 1) * size, lanes] = part_ref[pl.ds(theirs, size), :].astype(BF)
        high = rest.astype(BF)
        send[4 * size : 4 * size + 16, lanes] = high
        send[4 * size + 16 : 4 * size + 32, lanes] = (rest - high.astype(F32)).astype(BF)
        return carry

    lax.fori_loop(0, HEADS, one, 0)


def back_kernel(fw, fh, dy2, kern, gains, a1, dy1, own, other, acc_ref):
    slot = fw + TAIL
    count = dy1.shape[0]
    conv(lambda i: dy2[i * slot : i * slot + count], kern, acc_ref, count, True)
    grad = jnp.where(
        a1[2 * slot : 2 * slot + count] > 0.0, gains[0:1] * acc_ref[...], 0.0
    ).astype(BF)
    dy1[...] = grad
    acc_ref[...] = grad.astype(F32)
    rimmed(acc_ref, slot, slot, fw, fh, place()[3] == 0, own, other)


def input_kernel(fw, fh, dy1, kern, out, acc_ref):
    slot = fw + TAIL
    lead = slot // 2
    count = fh * slot + lead
    conv(
        lambda i: dy1[(i + 1) * slot - lead : (i + 1) * slot - lead + count],
        kern, acc_ref, count, True,
    )
    for r in range(fh):
        out[r] = acc_ref[lead + r * slot : lead + r * slot + fw]


def weight_kernel(fw, fh, forward, *refs):
    slot = fw + TAIL
    flat, wide = refs[0:4], refs[4:8]
    keep, send, turn_ref, wide_ref, shift_ref = refs[8:]
    core = place()[2]
    full = fh * slot
    length, lanes = wide_ref.shape
    lead = slot // 2
    for b in range(4):
        rows = []
        gap = jnp.zeros((TAIL, lanes), BF)
        for r in range(fh):
            rows += [flat[b][r], gap]
        turn_ref[:, b * full : (b + 1) * full] = jnp.concatenate(rows, axis=0).T
        wide_ref[0:lead] = jnp.zeros((lead, lanes), F32)
        for r in range(fh + 2):
            at = lead + r * slot
            wide_ref[at : at + fw] = wide[b][r].astype(F32)
            wide_ref[at + fw : at + slot] = jnp.zeros((TAIL, lanes), F32)
        for k, at in ((fh + 2, lead - 1), (fh + 3, lead + fw)):
            column = wide[b][k].astype(F32)
            for t in range(fh + 2):
                wide_ref[at + t * slot : at + t * slot + 1] = column[t : t + 1]
        value = wide_ref[...]
        shift_ref[0, b] = pltpu.roll(value, 1, 0).astype(BF)
        shift_ref[1, b] = value.astype(BF)
        shift_ref[2, b] = pltpu.roll(value, length - 1, 0).astype(BF)
    base = lead + slot
    size, part = keep.shape[2:]
    for i in range(3):
        for j in range(3):
            row, col = (i, j) if forward else (2 - i, 2 - j)
            at = base + (row - 1) * slot
            total = None
            for b in range(4):
                term = jnp.dot(
                    turn_ref[:, b * full : (b + 1) * full],
                    shift_ref[col, b, at : at + full],
                    preferred_element_type=F32,
                )
                total = term if total is None else total + term
            if forward:
                total = total.T
            total = total.astype(BF)
            for z in range(4):
                up, low = 2 * (z // 2) * size, (z % 2) * part
                even = total[up : up + size, low : low + part]
                odd = total[up + size : up + 2 * size, low : low + part]
                keep[z, 3 * i + j] = jnp.where(core == 0, even, odd)
                send[z, 3 * i + j] = jnp.where(core == 0, odd, even)


def pair_kernel(keep, got, own, *sends):
    spot = place()[1]
    for step in range(4):
        chunk = lax.rem(spot + step, 4)
        total = keep[chunk].astype(F32) + got[chunk].astype(F32)
        if step == 0:
            own[...] = total
        else:
            sends[step - 1][...] = total.astype(BF)


def sum_kernel(*refs):
    out = refs[8]
    for layer in range(2):
        own, *got = refs[4 * layer : 4 * layer + 4]
        total = own[...]
        for more in got:
            total += more[...].astype(F32)
        out[layer] = total.astype(BF)


def rest_out(send, at, small):
    high = small.astype(BF)
    send[at : at + 16] = high
    send[at + 16 : at + 32] = (small - high.astype(F32)).astype(BF)


def rest_in(got, at):
    return got[at : at + 16].astype(F32) + got[at + 16 : at + 32].astype(F32)


def head_pair_kernel(keep, small, got, own, rest, send):
    size = own.shape[0] // 2
    for m in range(4):
        total = keep[m * size : (m + 1) * size].astype(F32) + got[m * size : (m + 1) * size].astype(F32)
        at = (m // 2) * size
        if m % 2 == 0:
            own[at : at + size] = total
        else:
            send[at : at + size] = total.astype(BF)
    total = small[...] + rest_in(got, 4 * size)
    rest[...] = total
    rest_out(send, 2 * size, total)


def head_line_kernel(own, rest, got, own_out, rest_new, send):
    size = own_out.shape[0]
    own_out[...] = own[0:size] + got[0:size].astype(F32)
    send[0:size] = (own[size:] + got[size : 2 * size].astype(F32)).astype(BF)
    total = rest[...] + rest_in(got, 2 * size)
    rest_new[...] = total
    rest_out(send, size, total)


def head_plane_kernel(own, rest, got, own_out, rest_new, *sends):
    size, ho = own.shape
    part = ho // 4
    total = own[...] + got[0:size].astype(F32)
    small = rest[...] + rest_in(got, size)
    spot = place()[1]
    chunks = [total[:, c * part : (c + 1) * part] for c in range(4)]
    rest_new[...] = small
    for step in range(4):
        chunk = lax.rem(spot + step, 4)
        picked = chunks[0]
        for c in range(1, 4):
            picked = jnp.where(chunk == c, chunks[c], picked)
        if step == 0:
            own_out[...] = picked
        else:
            send = sends[step - 1]
            send[0:size] = picked.astype(BF)
            for c in range(4):
                rest_out(send, size + 32 * c, small[:, c * part : (c + 1) * part])


def head_sum_kernel(own, rest, first, second, third, out, small):
    size, part = own.shape
    total = own[...]
    for got in (first, second, third):
        total += got[0:size].astype(F32)
    out[...] = total
    for c in range(4):
        more = rest[:, c * part : (c + 1) * part]
        for got in (first, second, third):
            more += rest_in(got, size + 32 * c)
        small[:, c * part : (c + 1) * part] = more


def after(value, done):
    return lax.optimization_barrier((value, done))


def paired(near, far, axis):
    peers = lax.axis_size(axis)
    first = [(i, i ^ 1) for i in range(peers)]
    second = [(i, ((i + 1) ^ 1) - 1) for i in range(1, peers - 1)]
    return lax.ppermute(near, axis, first), lax.ppermute(far, axis, second)


def crossed(array, bits):
    peers = lax.axis_size("rows")
    return lax.ppermute(array, "rows", [(i, i ^ bits) for i in range(peers)])


def lined(arrays):
    return [
        lax.ppermute(a, "cols", [(i, (i + s + 1) % 4) for i in range(4)]) for s, a in enumerate(arrays)
    ]


def call(kernel, name, outs, args, scratch=(), flops=0, far=0, scalars=0):
    near = len(args) - far - scalars
    spaces = [pltpu.VMEM] * near + [pltpu.HBM] * far
    args = [pltpu.with_memory_space_constraint(a, s) for a, s in zip(args, spaces)] + list(args[near + far :])
    moved = sum(a.size * a.dtype.itemsize for a in args)
    return pl.pallas_call(
        kernel,
        out_shape=tuple(pltpu.VMEM(*out) for out in outs),
        in_specs=[VMEM] * near + [HBM] * far + [SMEM] * scalars,
        out_specs=(VMEM,) * len(outs),
        scratch_shapes=[pltpu.VMEM(*s) if isinstance(s, tuple) else s for s in scratch],
        compiler_params=pltpu.CompilerParams(vmem_limit_bytes=24 * 1024 * 1024),
        cost_estimate=pl.CostEstimate(flops=int(flops), bytes_accessed=moved, transcendentals=0),
        name=name,
    )(*args)


def shards(
    features, kernels, gains, shifts, head_weight, head_bias, head_scale, scale_id, valid, cotangent
):
    rows, cols = lax.axis_size("rows"), lax.axis_size("cols")
    feat, ct = features[0], cotangent[0]
    fh, fw, ch = feat.shape
    ho = ct.shape[2]
    slot = fw + TAIL
    span = fh * slot
    half = ch // 2
    size = ch // 8
    part = ho // 4
    flop = 2 * ch * ch * 9
    fast = rows == 8 and cols == 4

    core = ((fh, fw, half), BF)
    rows_f, rows_c = ((FH, fw, ch), BF), ((TH, fw, ho + 128), BF)
    edge = ((fh, TH, ho + 128), BF)
    feat, ct, code, f_near, f_far, c_near, c_far, edge0, edge1, feat_own, feat_other = call(
        functools.partial(prepare_kernel, fw, fh),
        "prepare",
        (((fh, fw, ch), BF), ((fh, fw, ho), BF), ((fh, fw, 128), BF))
        + (rows_f, rows_f, rows_c, rows_c, edge, edge, core, core),
        (feat, ct, scale_id[0], valid[0]),
        [DMA((2,))],
        far=2,
        scalars=2,
    )

    def load(layer, extra, done):
        args, done = after((kernels.reshape(2, 9, ch, ch), *extra), done)
        outs = [((9, ch, ch), BF)] + [(a.shape, BF) for a in extra]
        loaded = call(
            functools.partial(load_kernel, layer), f"load{layer}", outs, args, [DMA((2,))], far=len(args)
        )
        return loaded, done

    f_rows = paired(f_near, f_far, "rows")
    (taps1,), c_near = load(0, (), c_near)
    c_rows = paired(c_near, c_far, "rows")
    f_rows, taps1 = after(f_rows, taps1)
    edge = ((fh + 2 * FH, FH, ch), BF)
    f_near, f_far = call(
        functools.partial(lengthen_kernel, FH, 0), "lengthen", (edge, edge), (feat, *f_rows)
    )
    f_cols = paired(f_near, f_far, "cols")
    (taps2, head_weight), feat_own = load(1, (head_weight,), feat_own)
    feats = [feat_own, crossed(feat_own, 2), crossed(feat_other, 4), crossed(feat_other, 6)] if fast else []
    f_cols, taps2 = after(f_cols, taps2)
    edge = ((fh + 2 * TH, TH, ho + 128), BF)
    c_near, c_far = call(
        functools.partial(lengthen_parts_kernel, TH), "lengthen2", (edge, edge), (edge0, edge1, *c_rows)
    )
    c_cols = paired(c_near, c_far, "cols")

    n1 = (fh + 2 * FH - 1) * slot
    rim = ((fh + 4, fw, half), BF)
    f_cols, c_near = after(f_cols, c_near)
    a1, a_own, a_other = call(
        functools.partial(forward_kernel, fw, fh),
        "conv1",
        (((n1, ch), BF), rim, rim),
        (feat, *f_rows, *f_cols, taps1, gains, shifts),
        [((n1 + 2 * slot, ch), BF), ((n1, ch), F32)],
        n1 * flop,
    )
    if fast:
        acts = [a_own, crossed(a_own, 2), crossed(a_other, 4), crossed(a_other, 6)]
        a1, feats = after(a1, feats)

    n2 = (fh + 2 * TH + 1) * slot
    lo = (TH + 1) * slot
    head_out, dy2, dy2_own, dy2_other, turned, dh, gu, hot = call(
        functools.partial(head_kernel, fw, fh),
        "head",
        (((fh, fw, ho), BF), ((n2, ch), BF), core, core, ((ch, span), BF))
        + (((n2, ho), BF), ((n2, ho), BF), ((16, span), BF)),
        (a1, taps2, gains, shifts, head_weight, head_bias, head_scale, ct, code, *c_rows, *c_cols),
        [((n2, ch), F32), ((n2, ch), BF), ((n2, HC), BF), ((n2, 128), BF)]
        + [((2, n2, HC), F32), ((n2, HC), F32), ((n2, 128), BF)],
        n2 * (flop + 4 * ch * ho),
    )
    if fast:
        dy2s = [dy2_own, crossed(dy2_other, 2), crossed(dy2_own, 4), crossed(dy2_other, 6)]
        dy2, acts = after(dy2, acts)

    n3 = (fh + 3) * slot
    dy1, dy1_own, dy1_other = call(
        functools.partial(back_kernel, fw, fh),
        "back2",
        (((n3, ch), BF), rim, rim),
        (dy2, taps2, gains, a1),
        [((n3, ch), F32)],
        n3 * flop,
    )

    rest = ((16, ho), F32)

    def head_weights(turned):
        return call(
            functools.partial(head_weight_kernel, lo),
            "headweight",
            (((4 * size, ho), BF), ((4 * size + 32, ho), BF), rest),
            (turned, dh, gu, hot),
            [((ch, HC), F32)],
            2 * span * ch * ho,
        )

    def input_grad(dy1):
        (out,) = call(
            functools.partial(input_kernel, fw, fh),
            "back1",
            (((fh, fw, ch), F32),),
            (dy1, taps1),
            [((span + slot // 2, ch), F32)],
            span * flop,
        )
        return out

    if fast:
        dy1s = [dy1_own, crossed(dy1_other, 2), crossed(dy1_own, 4), crossed(dy1_other, 6)]
        turned, dy1_own = after(turned, dy1_own)
        hw_keep, hw_send, small = head_weights(turned)
        dy2s, hw_keep = after(dy2s, hw_keep)

        def grad_part(flat, wider, forward, name):
            parted = ((4, 9, size, half // 2), BF)
            length = (fh + 2) * slot + slot // 2
            return call(
                functools.partial(weight_kernel, fw, fh, forward),
                name,
                (parted, parted),
                (*flat, *wider),
                [((half, 4 * span), BF), ((length, half), F32), ((3, 4, length, half), BF)],
                span * flop,
            )

        chunk = (9, size, half // 2)

        def grad_pair(keep, got, name):
            own, *sends = call(
                pair_kernel, name, ((chunk, F32),) + ((chunk, BF),) * 3, (keep, got), flops=keep.size
            )
            return own, lined(sends)

        keep2, send2 = grad_part(dy2s, acts, True, "grad2")
        got2 = crossed(send2, 1)
        hw_got = crossed(hw_send, 1)
        dy1, keep2 = after(dy1, keep2)
        grad_features = input_grad(dy1)
        keep2, grad_features = after(keep2, grad_features)
        own2, lined2 = grad_pair(keep2, got2, "pair2")
        feats, own2 = after(feats, own2)
        keep1, send1 = grad_part(feats, dy1s, False, "grad1")
        got1 = crossed(send1, 1)
        hw_keep, keep1 = after(hw_keep, keep1)
        own, small, send = call(
            head_pair_kernel,
            "headpair",
            (((2 * size, ho), F32), rest, ((2 * size + 32, ho), BF)),
            (hw_keep, small, hw_got),
        )
        got = crossed(send, 2)
        keep1, own = after(keep1, own)
        own1, lined1 = grad_pair(keep1, got1, "pair1")
        own, own1 = after(own, own1)
        own, small, send = call(
            head_line_kernel,
            "headline",
            (((size, ho), F32), rest, ((size + 32, ho), BF)),
            (own, small, got),
        )
        got = crossed(send, 4)
        own, small, *sends = call(
            head_plane_kernel,
            "headplane",
            (((size, part), F32), rest) + (((size + 128, part), BF),) * 3,
            (own, small, got),
        )
        got = lined(sends)
        own2, own = after(own2, own)
        (total,) = call(sum_kernel, "sum", (((2,) + chunk, BF),), (own1, *lined1, own2, *lined2))
        pairs = []
        for r in range(8):
            for c in range(4):
                to_row = 4 * (r >> 2) + 2 * (c >> 1) + (r & 1)
                to_col = 2 * ((r >> 1) & 1) + (c & 1)
                pairs.append((4 * r + c, 4 * to_row + to_col))
        total = lax.ppermute(total, ("rows", "cols"), pairs)
        grad_kernels = total.astype(F32).reshape(2, 3, 3, size, half // 2)
        grad_head_weight, small = call(
            head_sum_kernel, "headsum", (((size, part), F32), rest), (own, small, *got)
        )
        grad_head_scale, grad_head_bias = small[:SCALES], small[SCALES]
    else:
        row = lax.axis_index("rows")
        grad_features = input_grad(dy1)
        hw_keep, hw_send, small = head_weights(turned)
        flat = jnp.pad(feat, ((0, 0), (0, TAIL), (0, 0))).reshape(span, ch)
        dy2_flat = dy2[(TH + 1) * slot :][:span].reshape(fh, slot, ch)[:, :fw]
        dy2_flat = jnp.pad(dy2_flat, ((0, 0), (0, TAIL), (0, 0))).reshape(span, ch)
        parts = []
        for left, right, first, sign in ((flat, jnp.pad(dy1, ((0, 8), (0, 0))), 2, -1), (a1, dy2_flat, 4, 1)):
            for i in (-1, 0, 1):
                for j in (-1, 0, 1):
                    at = (first + sign * i) * slot + sign * j
                    if sign < 0:
                        pair = (left, right[at : at + span])
                    else:
                        pair = (left[at : at + span], right)
                    parts.append(jnp.einsum("pc,pk->ck", *pair, preferred_element_type=F32).astype(BF))
        total = jnp.stack(parts).reshape(2, 3, 3, ch, ch)
        total = lax.psum_scatter(total, "cols", scatter_dimension=4, tiled=True)
        grad_kernels = lax.psum_scatter(
            total.astype(F32), "rows", scatter_dimension=3, tiled=True
        )
        at = (row >> 1) & 3
        order = [(at ^ m) * 2 for m in range(4)]
        hw_keep, hw_send = hw_keep.reshape(4, size, ho), hw_send[: 4 * size].reshape(4, size, ho)
        blocks = jnp.zeros((8, size, ho), BF)
        for m in range(4):
            blocks = lax.dynamic_update_slice(blocks, hw_keep[m : m + 1], (order[m] + (row & 1), 0, 0))
            blocks = lax.dynamic_update_slice(blocks, hw_send[m : m + 1], (order[m] + 1 - (row & 1), 0, 0))
        part = lax.psum_scatter(blocks.reshape(ch, ho), "cols", scatter_dimension=1, tiled=True)
        grad_head_weight = lax.psum_scatter(part.astype(F32), "rows", scatter_dimension=0, tiled=True)
        small = lax.psum(small[:4], ("rows", "cols"))
        grad_head_scale, grad_head_bias = small[:SCALES], small[SCALES]
    return (
        head_out[None],
        grad_features[None],
        grad_kernels,
        grad_head_weight,
        grad_head_bias,
        grad_head_scale,
    )


def solution(mesh):
    return jax.shard_map(
        shards,
        mesh=mesh,
        in_specs=(
            P(None, "rows", "cols", None),
            P(),
            P(),
            P(),
            P(),
            P(),
            P(),
            P(None, "rows", "cols"),
            P(None, "rows", "cols"),
            P(None, "rows", "cols", None),
        ),
        out_specs=(
            P(None, "rows", "cols", None),
            P(None, "rows", "cols", None),
            P(None, None, None, "rows", "cols"),
            P("rows", "cols"),
            P(),
            P(),
        ),
        check_vma=False,
    )
```

```python
import functools

import jax
import jax.numpy as jnp
from jax import lax
from jax.experimental import pallas as pl
from jax.experimental.pallas import tpu as pltpu
from jax.sharding import PartitionSpec as P

HC = 256
HEADS = 7
SCALES = 3
PBLK = 8
EPS = 1e-06

FH = 4
TH = 2
TAIL = 8

BF = jnp.bfloat16
F32 = jnp.float32
VMEM = pl.BlockSpec(memory_space=pltpu.VMEM)
HBM = pl.BlockSpec(memory_space=pltpu.HBM)
DMA = pltpu.SemaphoreType.DMA


def place():
    row, col = lax.axis_index("rows"), lax.axis_index("cols")
    return row, col, row & 1, (row >> 1) & 1, (row >> 2) & 1, (row >> 1) & 3


def in_image(first, count, slot, fw, fh):
    index = lax.broadcasted_iota(jnp.int32, (count, 1), 0)
    spot = lax.rem(index, slot)
    ahead = spot >= fw + TAIL // 2
    at_row, at_col = place()[:2]
    row = at_row * fh + lax.div(index, slot) + (first - FH - 1) + jnp.where(ahead, 1, 0)
    col = at_col * fw + jnp.where(ahead, spot - slot, spot)
    high, wide = lax.axis_size("rows") * fh, lax.axis_size("cols") * fw
    inside = (row >= 0) & (row < high) & (col >= 0) & (col < wide)
    return inside.astype(F32)


def conv(load, w_ref, acc_ref, count, back):
    for j in (1, 0, 2):
        total = None
        for i in range(3):
            weight = w_ref[3 * i + j]
            if back:
                term = lax.dot_general(
                    load(2 - i), weight, (((1,), (1,)), ((), ())), preferred_element_type=F32
                )
            else:
                term = jnp.dot(load(i), weight, preferred_element_type=F32)
            total = term if total is None else total + term
        if j == 1:
            acc_ref[...] = total
        else:
            step = 1 if (j == 0) != back else count - 1
            acc_ref[...] += pltpu.roll(total, step, 0)


def rimmed(src_ref, first, slot, fw, fh):
    for r in range(fh + 4):
        if r < fh + 2:
            part = src_ref[first + r * slot : first + r * slot + fw]
        else:
            at = first - 1 if r == fh + 2 else first + fw
            part = [src_ref[at + t * slot : at + t * slot + 1] for t in range(fh + 2)]
            part = jnp.concatenate(part + [jnp.zeros((fw - fh - 2, src_ref.shape[1]), F32)], axis=0)
        yield r, part.astype(BF)


def shares(values):
    part = values.shape[1] // 4
    cut = [values[:, c * part : (c + 1) * part] for c in range(4)]
    return jnp.concatenate([cut[0], cut[2]], axis=1), jnp.concatenate([cut[1], cut[3]], axis=1)


def put_shares(r, values, own, other):
    even, odd = shares(values)
    is_even = (place()[1] & 1) == 0
    own[r] = jnp.where(is_even, even, odd)
    other[r] = jnp.where(is_even, odd, even)


def wide_parts(values, code, ch):
    pixels, ho = values.shape
    whole = jnp.concatenate([values, code, jnp.zeros((pixels, -(ho + 128) % ch), BF)], axis=1)
    return [whole[:, at : at + ch] for at in range(0, whole.shape[1], ch)]


def prepare_kernel(
    fw, fh, feat_hbm, ct_hbm, ids_hbm, valid_hbm, feat, ct, code, near, far, edge0, edge1, ids, valid, sems
):
    moves = ((feat_hbm, feat), (ct_hbm, ct), (ids_hbm, ids), (valid_hbm, valid))
    moves = [pltpu.make_async_copy(src, dst, sems.at[n]) for n, (src, dst) in enumerate(moves)]
    for move in moves:
        move.start()
    for n in (2, 3, 0):
        moves[n].wait()
    ch = feat.shape[2]
    row, col, core, xbit, ybit, chip = place()
    levels = jnp.where(valid[0] == 1, ids[0] + 1, 0).astype(F32)
    for r in range(fh):
        b = r // PBLK
        pieces = [jnp.broadcast_to(levels[b : b + 1, c : c + 1], (PBLK, 128)) for c in range(fw // PBLK)]
        code[r] = jnp.concatenate(pieces, axis=0).astype(BF)
    for r in range(FH):
        top, bottom = feat[r], feat[fh - FH + r]
        near[r] = jnp.where(core == 0, bottom, top)
        far[r] = jnp.where(core == 0, top, bottom)
    pairs = FH // 2
    for r in range(fh):
        for p in range(pairs):
            edge0[r * pairs + p] = feat[r, 2 * p : 2 * p + 2]
            edge1[r * pairs + p] = feat[r, fw - FH + 2 * p : fw - FH + 2 * p + 2]
    moves[1].wait()
    for r in range(TH):
        tops = wide_parts(ct[r], code[r], ch)
        bottoms = wide_parts(ct[fh - TH + r], code[fh - TH + r], ch)
        for q, (top, bottom) in enumerate(zip(tops, bottoms)):
            near[FH + r * len(tops) + q] = jnp.where(core == 0, bottom, top)
            far[FH + r * len(tops) + q] = jnp.where(core == 0, top, bottom)
    for r in range(fh):
        for out, at in ((edge0, 0), (edge1, fw - TH)):
            parts = wide_parts(ct[r, at : at + TH], code[r, at : at + TH], ch)
            for q, part in enumerate(parts):
                out[fh * pairs + r * len(parts) + q] = part


def load_kernel(layer, src_hbm, *refs):
    count = (len(refs) - 1) // 2
    sems = refs[-1]
    extra = refs[: len(refs) // 2 - 1] if len(refs) > 2 else ()
    dst = refs[len(extra)]
    moves = [pltpu.make_async_copy(src_hbm.at[layer], dst, sems.at[0])]
    for n, src in enumerate(extra):
        moves.append(pltpu.make_async_copy(src, refs[len(extra) + 1 + n], sems.at[1 + n]))
    for move in moves:
        move.start()
    for move in moves:
        move.wait()


def lengthen_kernel(fh, edge0, edge1, near, far, out_near, out_far):
    fw = near.shape[1]
    pairs = FH // 2
    parts = (near.shape[0] - FH) // TH
    tall, thin = (fh + 2 * FH) * pairs, fh * pairs
    row, col, core = place()[:3]
    even = lax.rem(col, 2) == 0

    def put(at, first, last):
        out_near[at] = jnp.where(even, last, first)
        out_far[at] = jnp.where(even, first, last)

    for f_at, c_at, is_up in ((0, 0, True), (FH + fh, TH + fh, False)):
        other = core == 0 if is_up else core == 1
        for r in range(FH):
            for p in range(pairs):
                ends = []
                for col_at in (2 * p, fw - FH + 2 * p):
                    here = slice(col_at, col_at + 2)
                    ends.append(jnp.where(other, far[r, here], near[r, here]))
                put((f_at + r) * pairs + p, *ends)
        for r in range(TH * parts):
            ends = []
            for col_at in (0, fw - TH):
                here = slice(col_at, col_at + TH)
                ends.append(jnp.where(other, far[FH + r, here], near[FH + r, here]))
            put(tall + c_at * parts + r, *ends)
    for out, here, there in ((out_near, edge1, edge0), (out_far, edge0, edge1)):
        out[FH * pairs : (FH + fh) * pairs] = jnp.where(even, here[0:thin], there[0:thin])
        out[tall + TH * parts : tall + (TH + fh) * parts] = jnp.where(
            even, here[thin : thin + fh * parts], there[thin : thin + fh * parts]
        )


def forward_kernel(
    fw, fh, feat, r_near, r_far, c_near, c_far, kern, gains, shifts, act, rim, x_ref, acc_ref
):
    slot = fw + TAIL
    count = act.shape[0]
    ch = x_ref.shape[1]
    pairs = FH // 2
    row, col, core, xbit, ybit, chip = place()
    even = lax.rem(col, 2) == 0
    none = jnp.zeros((2, ch), BF)
    for s in range(fh + 2 * FH + 1):
        at = s * slot
        if s == 0:
            piece = jnp.zeros((fw, ch), BF)
        elif s <= FH:
            piece = jnp.where(core == 0, r_far[s - 1], r_near[s - 1])
        elif s <= FH + fh:
            piece = feat[s - 1 - FH]
        else:
            piece = jnp.where(core == 0, r_near[s - 1 - FH - fh], r_far[s - 1 - FH - fh])
        x_ref[at : at + fw] = piece
        tail = []
        for r, first, second in ((s - 1, c_near, c_far), (s, c_far, c_near)):
            for p in range(pairs):
                n = r * pairs + p
                tail.append(jnp.where(even, first[n], second[n]) if 0 <= r < fh + 2 * FH else none)
        x_ref[at + fw : at + slot] = jnp.concatenate(tail, axis=0)
    conv(lambda i: x_ref[i * slot : i * slot + count], kern, acc_ref, count, False)
    pre = gains[0:1] * acc_ref[...] + shifts[0:1]
    out = (jnp.maximum(pre, 0.0) * in_image(1, count, slot, fw, fh)).astype(BF)
    act[...] = out
    acc_ref[...] = out.astype(F32)
    for r, part in rimmed(acc_ref, 3 * slot, slot, fw, fh):
        rim[r] = part


def head_kernel(
    fw, fh, a1, kern, gains, shifts, hw_ref, bias, scale, ct, ct_code, r_near, r_far, c_near, c_far,
    head_out, dy, dy_own, dy_other, turned, dh_ref, gu_ref, hot,
    acc_ref, a2_ref, ct_ref, code_ref, h_ref, s_ref, level_ref,
):
    slot = fw + TAIL
    count, ch = dy.shape
    ho = ct.shape[2]
    rows = fh + 2 * TH + 1
    lo, hi = (TH + 1) * slot, (TH + 1 + fh) * slot
    row, col, core, xbit, ybit, chip = place()

    parts = -(-(ho + 128) // ch)
    thin = (fh + 2 * FH) * (FH // 2)
    even = lax.rem(col, 2) == 0

    def spread(dst, q, lanes, first):
        wide = dst.shape[1]
        dst[0:fw] = jnp.zeros((fw, wide), BF)
        none = jnp.zeros((TH, wide), BF)
        for s in range(rows):
            if 0 < s <= TH:
                at = FH + (s - 1) * parts + q
                dst[s * slot : s * slot + fw] = jnp.where(
                    core == 0, r_far[at, :, lanes], r_near[at, :, lanes]
                )
            elif TH < s <= TH + fh:
                dst[s * slot : s * slot + fw] = first(s - 1 - TH)
            elif s > 0:
                at = FH + (s - 1 - TH - fh) * parts + q
                dst[s * slot : s * slot + fw] = jnp.where(
                    core == 0, r_near[at, :, lanes], r_far[at, :, lanes]
                )
            right = left = none
            if s > 0:
                at = thin + (s - 1) * parts + q
                right = jnp.where(even, c_near[at, :, lanes], c_far[at, :, lanes])
            if s < rows - 1:
                at = thin + s * parts + q
                left = jnp.where(even, c_far[at, :, lanes], c_near[at, :, lanes])
            tail = [right, jnp.zeros((TAIL - 2 * TH, wide), BF), left]
            dst[s * slot + fw : (s + 1) * slot] = jnp.concatenate(tail, axis=0)

    conv(lambda i: a1[i * slot : i * slot + count], kern, acc_ref, count, False)
    act = jnp.maximum(gains[1:2] * acc_ref[...] + shifts[1:2], 0.0).astype(BF)
    a2_ref[...] = act
    index = lax.broadcasted_iota(jnp.int32, (hi - lo, 1), 0)
    inner = lax.rem(index, slot) < fw
    turned[...] = jnp.where(inner, act[lo:hi], jnp.zeros_like(act[lo:hi])).T
    spread(code_ref, ho // ch, pl.ds(ho % ch, 128), lambda r: ct_code[r])
    code = code_ref[...].astype(F32)
    lane = lax.broadcasted_iota(jnp.int32, (count, 128), 1)
    turn = jnp.where(lane < SCALES, lane, jnp.where(lane < 2 * SCALES, lane - SCALES, lane - 2 * SCALES))
    wanted = jnp.where(lane < 3 * SCALES, turn + 1, -1).astype(F32)
    level = jnp.where(code == wanted, 1.0, 0.0)
    level_ref[...] = level.astype(BF)
    core_level = jnp.where(lane[lo:hi] < SCALES, level[lo:hi], jnp.where(lane[lo:hi] == SCALES, 1.0, 0.0))
    hot[...] = jnp.where(inner, core_level, 0.0).astype(BF).T[: hot.shape[0]]

    def product(g):
        lanes = pl.ds(pl.multiple_of(jnp.minimum(g, HEADS - 1) * HC, HC), HC)
        h_ref[lax.rem(g, 2)] = jnp.dot(a2_ref[...], hw_ref[:, lanes], preferred_element_type=F32)

    product(0)
    block = count // rows * 3

    def one(g, carry):
        lanes = pl.ds(pl.multiple_of(g * HC, HC), HC)
        product(g + 1)
        inside = pl.ds(pl.multiple_of(lax.rem(g * HC, ch), HC), HC)
        spread(ct_ref, lax.div(g * HC, ch), inside, lambda r: ct[r, :, lanes])
        whole = scale[:, lanes]
        terms = []
        for _ in range(3):
            term = whole.astype(BF)
            terms.append(term.astype(F32))
            whole = whole - terms[-1]
        terms.append(jnp.zeros((128 - 3 * SCALES, HC), F32))
        terms = jnp.concatenate(terms, axis=0).astype(BF)
        s_ref[...] = jnp.dot(level_ref[...], terms, preferred_element_type=F32)
        offset = bias[lanes]
        for at in range(0, count, block):
            here = slice(at, at + block)
            h = h_ref[lax.rem(g, 2), here] + offset
            inv = lax.rsqrt(jnp.sum(h * h, axis=1, keepdims=True) + EPS)
            u = h * inv
            s = s_ref[here]
            up = ct_ref[here].astype(F32)
            du = up * s
            along = jnp.sum(du * u, axis=1, keepdims=True)
            dh_ref[here, lanes] = (inv * (du - u * along)).astype(BF)
            gu_ref[here, lanes] = (up * u).astype(BF)
            out = (s * u).astype(BF)
            for r in range(at // slot, (at + block) // slot):
                if TH + 1 <= r < TH + 1 + fh:
                    head_out[r - TH - 1, :, lanes] = out[r * slot - at : r * slot - at + fw]
        return carry

    lax.fori_loop(0, HEADS, one, 0)
    acc_ref[...] = lax.dot_general(
        dh_ref[...], hw_ref[...], (((1,), (1,)), ((), ())), preferred_element_type=F32
    )
    grad = jnp.where(a2_ref[...] > 0.0, gains[1:2] * acc_ref[...], 0.0).astype(BF)
    dy[...] = grad
    for r in range(fh):
        at = lo + r * slot
        put_shares(r, grad[at : at + fw], dy_own, dy_other)


def head_weight_kernel(lo, turned, dh_ref, gu_ref, hot, keep, send, small, part_ref):
    size = keep.shape[0] // 4
    span = turned.shape[1]
    row, col, core, xbit, ybit, chip = place()

    def one(g, carry):
        lanes = pl.ds(pl.multiple_of(g * HC, HC), HC)
        dh = dh_ref[lo : lo + span, lanes]
        part_ref[...] = jnp.dot(turned[...], dh, preferred_element_type=F32)
        scale_part = jnp.dot(hot[...], gu_ref[lo : lo + span, lanes], preferred_element_type=F32)
        bias_part = jnp.dot(hot[...], dh, preferred_element_type=F32)
        pick = lax.broadcasted_iota(jnp.int32, scale_part.shape, 0)
        rest = jnp.where(pick < SCALES, scale_part, bias_part)[:8]
        small[:, lanes] = rest
        for m in range(4):
            block = 2 * lax.bitwise_xor(chip, m)
            mine = pl.multiple_of((block + core) * size, size)
            theirs = pl.multiple_of((block + 1 - core) * size, size)
            keep[m * size : (m + 1) * size, lanes] = part_ref[pl.ds(mine, size), :].astype(BF)
            send[m * size : (m + 1) * size, lanes] = part_ref[pl.ds(theirs, size), :].astype(BF)
        send[4 * size : 4 * size + 16, lanes] = two_terms(rest)
        return carry

    lax.fori_loop(0, HEADS, one, 0)


def back_kernel(fw, fh, dy2, kern, gains, a1, dy1, own, other, acc_ref):
    slot = fw + TAIL
    count = dy1.shape[0]
    conv(lambda i: dy2[i * slot : i * slot + count], kern, acc_ref, count, True)
    grad = jnp.where(
        a1[2 * slot : 2 * slot + count] > 0.0, gains[0:1] * acc_ref[...], 0.0
    ).astype(BF)
    dy1[...] = grad
    acc_ref[...] = grad.astype(F32)
    for r, part in rimmed(acc_ref, slot, slot, fw, fh):
        put_shares(r, part, own, other)


def input_kernel(fw, fh, dy1, kern, out, acc_ref):
    slot = fw + TAIL
    lead = slot // 2
    count = fh * slot + lead
    conv(
        lambda i: dy1[(i + 1) * slot - lead : (i + 1) * slot - lead + count],
        kern, acc_ref, count, True,
    )
    for r in range(fh):
        out[r] = acc_ref[lead + r * slot : lead + r * slot + fw]


def weight_kernel(fw, fh, forward, flat0, flat1, wide0, wide1, keep, send, turn_ref, wide_ref, shift_ref, part_ref):
    slot = fw + TAIL
    core, chip = place()[2], place()[5]
    full = fh * slot
    length, lanes = wide_ref.shape
    lead = slot // 2
    for b, (flat, wide) in enumerate(((flat0, wide0), (flat1, wide1))):
        rows = []
        gap = jnp.zeros((TAIL, flat.shape[2]), BF)
        for r in range(fh):
            rows += [flat[r], gap]
        turn_ref[:, b * full : (b + 1) * full] = jnp.concatenate(rows, axis=0).T
        wide_ref[0:lead] = jnp.zeros((lead, lanes), F32)
        for r in range(fh + 2):
            at = lead + r * slot
            wide_ref[at : at + fw] = wide[r].astype(F32)
            wide_ref[at + fw : at + slot] = jnp.zeros((TAIL, lanes), F32)
        for k, at in ((fh + 2, lead - 1), (fh + 3, lead + fw)):
            column = wide[k].astype(F32)
            for t in range(fh + 2):
                wide_ref[at + t * slot : at + t * slot + 1] = column[t : t + 1]
        value = wide_ref[...]
        shift_ref[0, b] = pltpu.roll(value, 1, 0).astype(BF)
        shift_ref[1, b] = value.astype(BF)
        shift_ref[2, b] = pltpu.roll(value, length - 1, 0).astype(BF)
    base = lead + slot
    size = keep.shape[2]
    for i in range(3):
        for j in range(3):
            row, col = (i, j) if forward else (2 - i, 2 - j)
            at = base + (row - 1) * slot
            total = None
            for b in range(2):
                term = jnp.dot(
                    turn_ref[:, b * full : (b + 1) * full],
                    shift_ref[col, b, at : at + full],
                    preferred_element_type=F32,
                )
                total = term if total is None else total + term
            part_ref[...] = total.T if forward else total
            for m in range(4):
                block = 2 * lax.bitwise_xor(chip, m)
                mine = pl.multiple_of((block + core) * size, size)
                theirs = pl.multiple_of((block + 1 - core) * size, size)
                keep[m, 3 * i + j] = part_ref[pl.ds(mine, size), :].astype(BF)
                send[m, 3 * i + j] = part_ref[pl.ds(theirs, size), :].astype(BF)


def pair_kernel(order, keep, got, own, send):
    for n, m in enumerate(order):
        total = keep[m].astype(F32) + got[m].astype(F32)
        if n < 2:
            own[n] = total
        else:
            send[n - 2] = total.astype(BF)


def line_kernel(own, got, out, send):
    out[...] = own[0] + got[0].astype(F32)
    send[...] = (own[1] + got[1].astype(F32)).astype(BF)


def plane_kernel(own, got, out, send):
    part = out.shape[2]
    high = (place()[1] >> 1) & 1
    for tap in range(own.shape[0]):
        total = own[tap] + got[tap].astype(F32)
        left, right = total[:, :part], total[:, part:]
        out[tap] = jnp.where(high == 0, left, right)
        send[tap] = jnp.where(high == 0, right, left).astype(BF)


def final_kernel(own1, got1, own2, got2, out):
    out[0] = own1[...] + got1[...].astype(F32)
    out[1] = own2[...] + got2[...].astype(F32)


def two_terms(values):
    high = values.astype(BF).astype(F32)
    return jnp.concatenate([high, values - high], axis=0).astype(BF)


def rest_in(got, at):
    terms = got[at : at + 16].astype(F32)
    return terms[:8] + terms[8:]


def head_pair_kernel(keep, small, got, own, rest, send):
    size = own.shape[0] // 2
    for m in range(4):
        here = slice(m * size, (m + 1) * size)
        total = keep[here].astype(F32) + got[here].astype(F32)
        at = (m % 2) * size
        if m < 2:
            own[at : at + size] = total
        else:
            send[at : at + size] = total.astype(BF)
    total = small[...] + rest_in(got, 4 * size)
    rest[...] = total
    send[2 * size : 2 * size + 16] = two_terms(total)


def head_line_kernel(own, rest, got, own_out, rest_new, send):
    size = own_out.shape[0]
    own_out[...] = own[0:size] + got[0:size].astype(F32)
    send[0:size] = (own[size:] + got[size : 2 * size].astype(F32)).astype(BF)
    total = rest[...] + rest_in(got, 2 * size)
    rest_new[...] = total
    send[size : size + 16] = two_terms(total)


def head_plane_kernel(own, rest, got, own_out, rest_new, send):
    size, ho = own.shape
    part = ho // 4
    low = place()[1] & 1
    total = own[...] + got[0:size].astype(F32)
    chunks = [total[:, c * part : (c + 1) * part] for c in range(4)]
    small = rest[...] + rest_in(got, size)
    rest_new[...] = small
    terms = two_terms(small)
    for m in range(2):
        even, odd = chunks[2 * m], chunks[2 * m + 1]
        lanes = slice(m * part, (m + 1) * part)
        own_out[m] = jnp.where(low == 0, even, odd)
        send[0:size, lanes] = jnp.where(low == 0, odd, even).astype(BF)
        send[size + 16 * m : size + 16 * m + 16] = terms[:, 2 * m * part : 2 * (m + 1) * part]


def head_middle_kernel(own, rest, got, own_out, rest_new, send):
    size, part = own_out.shape
    high = (place()[1] >> 1) & 1
    totals = [own[m] + got[0:size, m * part : (m + 1) * part].astype(F32) for m in range(2)]
    own_out[...] = jnp.where(high == 0, totals[0], totals[1])
    send[0:size] = jnp.where(high == 0, totals[1], totals[0]).astype(BF)
    for m in range(2):
        lanes = slice(2 * m * part, 2 * (m + 1) * part)
        small = rest[:, lanes] + rest_in(got, size + 16 * m)
        rest_new[:, lanes] = small
        terms = two_terms(small)
        for d in range(2):
            at = size + 16 * (2 * m + d)
            send[at : at + 16] = terms[:, d * part : (d + 1) * part]


def head_last_kernel(own, rest, got, out, scale, bias):
    size, part = own.shape
    out[...] = own[...] + got[0:size].astype(F32)
    for c in range(4):
        lanes = slice(c * part, (c + 1) * part)
        small = rest[:, lanes] + rest_in(got, size + 16 * c)
        scale[:, lanes] = small[:SCALES]
        bias[:, lanes] = small[SCALES : SCALES + 1]


def after(value, done):
    return lax.optimization_barrier((value, done))


def paired(near, far, axis):
    peers = lax.axis_size(axis)
    first = [(i, i ^ 1) for i in range(peers)]
    second = [(i, ((i + 1) ^ 1) - 1) for i in range(1, peers - 1)]
    return lax.ppermute(near, axis, first), lax.ppermute(far, axis, second)


def crossed(array, bits):
    peers = lax.axis_size("rows")
    return lax.ppermute(array, "rows", [(i, i ^ bits) for i in range(peers)])


def across(array, bits):
    peers = lax.axis_size("cols")
    return lax.ppermute(array, "cols", [(i, i ^ bits) for i in range(peers)])


def call(kernel, name, outs, args, scratch=(), far=0):
    near = len(args) - far
    spaces = [pltpu.VMEM] * near + [pltpu.HBM] * far
    args = [pltpu.with_memory_space_constraint(a, s) for a, s in zip(args, spaces)]
    return pl.pallas_call(
        kernel,
        out_shape=tuple(pltpu.VMEM(*out) for out in outs),
        in_specs=[VMEM] * near + [HBM] * far,
        out_specs=(VMEM,) * len(outs),
        scratch_shapes=[pltpu.VMEM(*s) if isinstance(s, tuple) else s for s in scratch],
        compiler_params=pltpu.CompilerParams(vmem_limit_bytes=24 * 1024 * 1024),
        cost_estimate=pl.CostEstimate(flops=10**10, bytes_accessed=0, transcendentals=0),
        name=name,
    )(*args)


def shards(
    features, kernels, gains, shifts, head_weight, head_bias, head_scale, scale_id, valid, cotangent
):
    rows, cols = lax.axis_size("rows"), lax.axis_size("cols")
    feat, ct = features[0], cotangent[0]
    fh, fw, ch = feat.shape
    ho = ct.shape[2]
    slot = fw + TAIL
    span = fh * slot
    half = ch // 2
    size = ch // 8
    part = ho // 4
    fast = rows == 8 and cols == 4

    parts = -(-(ho + 128) // ch)
    message = ((FH + TH * parts, fw, ch), BF)
    edge = ((fh * (FH // 2 + parts), 2, ch), BF)
    feat, ct, code, near, far, edge0, edge1 = call(
        functools.partial(prepare_kernel, fw, fh),
        "prepare",
        (((fh, fw, ch), BF), ((fh, fw, ho), BF), ((fh, fw, 128), BF), message, message, edge, edge),
        (feat, ct, scale_id, valid),
        [pltpu.VMEM(scale_id.shape, jnp.int32), pltpu.VMEM(valid.shape, jnp.int32), DMA((4,))],
        far=4,
    )

    def load(layer, extra, done):
        args, done = after((kernels.reshape(2, 9, ch, ch), *extra), done)
        outs = [((9, ch, ch), BF)] + [(a.shape, BF) for a in extra]
        loaded = call(
            functools.partial(load_kernel, layer), f"load{layer}", outs, args, [DMA((2,))], far=len(args)
        )
        return loaded, done

    by_row = paired(near, far, "rows")
    (taps1,), edge0 = load(0, (), edge0)
    edge0, taps1 = after(edge0, taps1)
    edge = (((fh + 2 * FH) * (FH // 2) + (fh + 2 * TH) * parts, 2, ch), BF)
    near, far = call(
        functools.partial(lengthen_kernel, fh), "lengthen", (edge, edge), (edge0, edge1, *by_row)
    )
    by_col = paired(near, far, "cols")
    (taps2, head_weight), near = load(1, (head_weight,), near)
    by_col, taps2 = after(by_col, taps2)

    core = ((fh, fw, half), BF)
    n1 = (fh + 2 * FH - 1) * slot
    a1, a1_rim = call(
        functools.partial(forward_kernel, fw, fh),
        "conv1",
        (((n1, ch), BF), ((fh + 4, fw, ch), BF)),
        (feat, *by_row, *by_col, taps1, gains, shifts),
        [((n1 + 2 * slot, ch), BF), ((n1, ch), F32)],
    )
    if fast:
        feats = [feat, across(feat, 1)]
        acts = [a1_rim, across(a1_rim, 1)]

    n2 = (fh + 2 * TH + 1) * slot
    lo = (TH + 1) * slot
    head_out, dy2, dy2_own, dy2_other, turned, dh, gu, hot = call(
        functools.partial(head_kernel, fw, fh),
        "head",
        (((fh, fw, ho), BF), ((n2, ch), BF), core, core, ((ch, span), BF))
        + (((n2, ho), BF), ((n2, ho), BF), ((16, span), BF)),
        (a1, taps2, gains, shifts, head_weight, head_bias, head_scale, ct, code, *by_row, *by_col),
        [((n2, ch), F32), ((n2, ch), BF), ((n2, HC), BF), ((n2, 128), BF)]
        + [((2, n2, HC), F32), ((n2, HC), F32), ((n2, 128), BF)],
    )
    if fast:
        dy2s = [dy2_own, across(dy2_other, 1)]
        turned, (feats, acts) = after(turned, (feats, acts))

    rest = ((8, ho), F32)
    hw_keep, hw_send, small = call(
        functools.partial(head_weight_kernel, lo),
        "headweight",
        (((4 * size, ho), BF), ((4 * size + 16, ho), BF), rest),
        (turned, dh, gu, hot),
        [((ch, HC), F32)],
    )
    dy2, small = after(dy2, small)

    n3 = (fh + 3) * slot
    rim = ((fh + 4, fw, half), BF)
    dy1, dy1_own, dy1_other = call(
        functools.partial(back_kernel, fw, fh),
        "back2",
        (((n3, ch), BF), rim, rim),
        (dy2, taps2, gains, a1),
        [((n3, ch), F32)],
    )

    def input_grad(dy1):
        (out,) = call(
            functools.partial(input_kernel, fw, fh),
            "back1",
            (((fh, fw, ch), F32),),
            (dy1, taps1),
            [((span + slot // 2, ch), F32)],
        )
        return out

    if fast:
        hw_got = crossed(hw_send, 1)
        dy1s = [dy1_own, across(dy1_other, 1)]

        def grad_part(flat, wide, forward, name):
            parted = ((4, 9, size, half), BF)
            length = (fh + 2) * slot + slot // 2
            lanes = wide[0].shape[2]
            return call(
                functools.partial(weight_kernel, fw, fh, forward),
                name,
                (parted, parted),
                (*flat, *wide),
                [((flat[0].shape[2], 2 * span), BF), ((length, lanes), F32), ((3, 2, length, lanes), BF)]
                + [((ch, half), F32)],
            )

        block = (9, size, half)
        blocks = (2,) + block
        chunk = (9, size, half // 2)
        halves = ((blocks, F32), (blocks, BF))
        lines = ((block, F32), (block, BF))
        chunks = ((chunk, F32), (chunk, BF))

        dy2s, dy1_own = after(dy2s, dy1_own)
        keep2, send2 = grad_part(dy2s, acts, True, "grad2")
        got2 = crossed(send2, 1)
        hw_keep, keep2 = after(hw_keep, keep2)
        own, small, send = call(
            head_pair_kernel,
            "headpair",
            (((2 * size, ho), F32), rest, ((2 * size + 16, ho), BF)),
            (hw_keep, small, hw_got),
        )
        got = crossed(send, 4)
        feats, own = after(feats, own)
        keep1, send1 = grad_part(feats, dy1s, False, "grad1")
        got1 = crossed(send1, 1)
        keep2, keep1 = after(keep2, keep1)
        own2, send2 = call(functools.partial(pair_kernel, (0, 2, 1, 3)), "pair2", halves, (keep2, got2))
        got2 = crossed(send2, 2)
        dy1, own2 = after(dy1, own2)
        grad_features = input_grad(dy1)
        own, grad_features = after(own, grad_features)
        own, small, send = call(
            head_line_kernel, "headline", (((size, ho), F32), rest, ((size + 16, ho), BF)), (own, small, got)
        )
        got = crossed(send, 2)
        keep1, own = after(keep1, own)
        own1, send1 = call(functools.partial(pair_kernel, (0, 1, 2, 3)), "pair1", halves, (keep1, got1))
        got1 = crossed(send1, 4)
        own2, own1 = after(own2, own1)
        own2, send2 = call(line_kernel, "line2", lines, (own2, got2))
        got2 = crossed(send2, 4)
        own, own2 = after(own, own2)
        own, small, send = call(
            head_plane_kernel,
            "headplane",
            (((2, size, part), F32), rest, ((size + 32, 2 * part), BF)),
            (own, small, got),
        )
        got = across(send, 1)
        own1, own = after(own1, own)
        own1, send1 = call(line_kernel, "line1", lines, (own1, got1))
        got1 = crossed(send1, 2)
        own2, own1 = after(own2, own1)
        own2, send2 = call(plane_kernel, "plane2", chunks, (own2, got2))
        got2 = across(send2, 2)
        own, own2 = after(own, own2)
        own, small, send = call(
            head_middle_kernel,
            "headmiddle",
            (((size, part), F32), rest, ((size + 64, part), BF)),
            (own, small, got),
        )
        got = across(send, 2)
        own1, own = after(own1, own)
        own1, send1 = call(plane_kernel, "plane1", chunks, (own1, got1))
        got1 = across(send1, 2)
        own, own1 = after(own, own1)
        grad_head_weight, grad_head_scale, grad_head_bias = call(
            head_last_kernel,
            "headlast",
            (((size, part), F32), ((SCALES, ho), F32), ((1, ho), F32)),
            (own, small, got),
        )
        grad_head_bias = grad_head_bias[0]
        own1, grad_head_weight = after(own1, grad_head_weight)
        (total,) = call(final_kernel, "final", (((2,) + chunk, F32),), (own1, got1, own2, got2))
        grad_kernels = total.reshape(2, 3, 3, size, half // 2)
    else:
        row = lax.axis_index("rows")
        grad_features = input_grad(dy1)
        flat = jnp.pad(feat, ((0, 0), (0, TAIL), (0, 0))).reshape(span, ch)
        dy2_flat = dy2[(TH + 1) * slot :][:span].reshape(fh, slot, ch)[:, :fw]
        dy2_flat = jnp.pad(dy2_flat, ((0, 0), (0, TAIL), (0, 0))).reshape(span, ch)
        parts = []
        for left, right, first, sign in ((flat, jnp.pad(dy1, ((0, 8), (0, 0))), 2, -1), (a1, dy2_flat, 4, 1)):
            for i in (-1, 0, 1):
                for j in (-1, 0, 1):
                    at = (first + sign * i) * slot + sign * j
                    if sign < 0:
                        pair = (left, right[at : at + span])
                    else:
                        pair = (left[at : at + span], right)
                    parts.append(jnp.einsum("pc,pk->ck", *pair, preferred_element_type=F32).astype(BF))
        total = jnp.stack(parts).reshape(2, 3, 3, ch, ch)
        total = lax.psum_scatter(total, "cols", scatter_dimension=4, tiled=True)
        grad_kernels = lax.psum_scatter(
            total.astype(F32), "rows", scatter_dimension=3, tiled=True
        )
        at = (row >> 1) & 3
        order = [(at ^ m) * 2 for m in range(4)]
        hw_keep, hw_send = hw_keep.reshape(4, size, ho), hw_send[: 4 * size].reshape(4, size, ho)
        blocks = jnp.zeros((8, size, ho), BF)
        for m in range(4):
            blocks = lax.dynamic_update_slice(blocks, hw_keep[m : m + 1], (order[m] + (row & 1), 0, 0))
            blocks = lax.dynamic_update_slice(blocks, hw_send[m : m + 1], (order[m] + 1 - (row & 1), 0, 0))
        part = lax.psum_scatter(blocks.reshape(ch, ho), "cols", scatter_dimension=1, tiled=True)
        grad_head_weight = lax.psum_scatter(part.astype(F32), "rows", scatter_dimension=0, tiled=True)
        small = lax.psum(small[:4], ("rows", "cols"))
        grad_head_scale, grad_head_bias = small[:SCALES], small[SCALES]
    return (
        head_out[None],
        grad_features[None],
        grad_kernels,
        grad_head_weight,
        grad_head_bias,
        grad_head_scale,
    )


def solution(mesh):
    return jax.shard_map(
        shards,
        mesh=mesh,
        in_specs=(
            P(None, "rows", "cols", None),
            P(),
            P(),
            P(),
            P(),
            P(),
            P(),
            P(None, "rows", "cols"),
            P(None, "rows", "cols"),
            P(None, "rows", "cols", None),
        ),
        out_specs=(
            P(None, "rows", "cols", None),
            P(None, "rows", "cols", None),
            P(None, None, None, "rows", "cols"),
            P("rows", "cols"),
            P(),
            P(),
        ),
        check_vma=False,
    )
```

```python
import functools

import jax
import jax.numpy as jnp
from jax import lax
from jax.experimental import pallas as pl
from jax.experimental.pallas import tpu as pltpu
from jax.sharding import PartitionSpec as P

HC = 256
HEADS = 7
SCALES = 3
PBLK = 8
EPS = 1e-06

FH = 4
TH = 2
TAIL = 8

BF = jnp.bfloat16
F32 = jnp.float32
VMEM = pl.BlockSpec(memory_space=pltpu.VMEM)
HBM = pl.BlockSpec(memory_space=pltpu.HBM)
DMA = pltpu.SemaphoreType.DMA

ORDER = (
    "back2", "headweight", "grad2", "grad1", "pair2", "headpair",
    "pair1", "back1", "line2", "headline", "line1", "headplane",
    "plane1", "headmiddle", "plane2", "final", "headlast",
)
EARLY = {}
COSTS = {'headweight': 0, 'back2': 3000000000, 'grad2': 3000000000, 'grad1': 10000000000, 'headpair': 0, 'pair2': 20000000000, 'pair1': 100000000, 'back1': 1000000000, 'headline': 0, 'line2': 1000000000, 'headplane': 3000000000, 'line1': 0, 'headmiddle': 0, 'plane2': 1000000000, 'plane1': 3000000000, 'headlast': 3000000000, 'final': 20000000000, 'prepare': 1000000000, 'load0': 100000000, 'lengthen': 20000000000, 'load1': 0, 'conv1': 50000000000, 'head': 10000000000}


def place():
    row, col = lax.axis_index("rows"), lax.axis_index("cols")
    return row, col, row & 1, (row >> 1) & 1, (row >> 2) & 1, (row >> 1) & 3


def in_image(first, count, slot, fw, fh):
    index = lax.broadcasted_iota(jnp.int32, (count, 1), 0)
    spot = lax.rem(index, slot)
    ahead = spot >= fw + TAIL // 2
    at_row, at_col = place()[:2]
    row = at_row * fh + lax.div(index, slot) + (first - FH - 1) + jnp.where(ahead, 1, 0)
    col = at_col * fw + jnp.where(ahead, spot - slot, spot)
    high, wide = lax.axis_size("rows") * fh, lax.axis_size("cols") * fw
    inside = (row >= 0) & (row < high) & (col >= 0) & (col < wide)
    return inside.astype(F32)


def conv(load, w_ref, acc_ref, count, back):
    for j in (1, 0, 2):
        total = None
        for i in range(3):
            weight = w_ref[3 * i + j]
            if back:
                term = lax.dot_general(
                    load(2 - i), weight, (((1,), (1,)), ((), ())), preferred_element_type=F32
                )
            else:
                term = jnp.dot(load(i), weight, preferred_element_type=F32)
            total = term if total is None else total + term
        if j == 1:
            acc_ref[...] = total
        else:
            step = 1 if (j == 0) != back else count - 1
            acc_ref[...] += pltpu.roll(total, step, 0)


def rimmed(src_ref, first, slot, fw, fh):
    for r in range(fh + 4):
        if r < fh + 2:
            part = src_ref[first + r * slot : first + r * slot + fw]
        else:
            at = first - 1 if r == fh + 2 else first + fw
            part = [src_ref[at + t * slot : at + t * slot + 1] for t in range(fh + 2)]
            part = jnp.concatenate(part + [jnp.zeros((fw - fh - 2, src_ref.shape[1]), F32)], axis=0)
        yield r, part.astype(BF)


def shares(values):
    part = values.shape[1] // 4
    cut = [values[:, c * part : (c + 1) * part] for c in range(4)]
    return jnp.concatenate([cut[0], cut[2]], axis=1), jnp.concatenate([cut[1], cut[3]], axis=1)


def put_shares(r, values, own, other):
    even, odd = shares(values)
    is_even = (place()[1] & 1) == 0
    own[r] = jnp.where(is_even, even, odd)
    other[r] = jnp.where(is_even, odd, even)


def wide_parts(values, code, ch):
    pixels, ho = values.shape
    whole = jnp.concatenate([values, code, jnp.zeros((pixels, -(ho + 128) % ch), BF)], axis=1)
    return [whole[:, at : at + ch] for at in range(0, whole.shape[1], ch)]


def prepare_kernel(
    fw, fh, feat_hbm, ct_hbm, ids_hbm, valid_hbm, feat, ct, code, near, far, edge0, edge1, ids, valid, sems
):
    moves = ((feat_hbm, feat), (ct_hbm, ct), (ids_hbm, ids), (valid_hbm, valid))
    moves = [pltpu.make_async_copy(src, dst, sems.at[n]) for n, (src, dst) in enumerate(moves)]
    for move in moves:
        move.start()
    for n in (2, 3, 0):
        moves[n].wait()
    ch = feat.shape[2]
    row, col, core, xbit, ybit, chip = place()
    levels = jnp.where(valid[0] == 1, ids[0] + 1, 0).astype(F32)
    for r in range(fh):
        b = r // PBLK
        pieces = [jnp.broadcast_to(levels[b : b + 1, c : c + 1], (PBLK, 128)) for c in range(fw // PBLK)]
        code[r] = jnp.concatenate(pieces, axis=0).astype(BF)
    for r in range(FH):
        top, bottom = feat[r], feat[fh - FH + r]
        near[r] = jnp.where(core == 0, bottom, top)
        far[r] = jnp.where(core == 0, top, bottom)
    pairs = FH // 2
    for r in range(fh):
        for p in range(pairs):
            edge0[r * pairs + p] = feat[r, 2 * p : 2 * p + 2]
            edge1[r * pairs + p] = feat[r, fw - FH + 2 * p : fw - FH + 2 * p + 2]
    moves[1].wait()
    for r in range(TH):
        tops = wide_parts(ct[r], code[r], ch)
        bottoms = wide_parts(ct[fh - TH + r], code[fh - TH + r], ch)
        for q, (top, bottom) in enumerate(zip(tops, bottoms)):
            near[FH + r * len(tops) + q] = jnp.where(core == 0, bottom, top)
            far[FH + r * len(tops) + q] = jnp.where(core == 0, top, bottom)
    for r in range(fh):
        for out, at in ((edge0, 0), (edge1, fw - TH)):
            parts = wide_parts(ct[r, at : at + TH], code[r, at : at + TH], ch)
            for q, part in enumerate(parts):
                out[fh * pairs + r * len(parts) + q] = part


def load_kernel(layer, src_hbm, *refs):
    count = (len(refs) - 1) // 2
    sems = refs[-1]
    extra = refs[: len(refs) // 2 - 1] if len(refs) > 2 else ()
    dst = refs[len(extra)]
    moves = [pltpu.make_async_copy(src_hbm.at[layer], dst, sems.at[0])]
    for n, src in enumerate(extra):
        moves.append(pltpu.make_async_copy(src, refs[len(extra) + 1 + n], sems.at[1 + n]))
    for move in moves:
        move.start()
    for move in moves:
        move.wait()


def lengthen_kernel(fh, edge0, edge1, near, far, out_near, out_far):
    fw = near.shape[1]
    pairs = FH // 2
    parts = (near.shape[0] - FH) // TH
    tall, thin = (fh + 2 * FH) * pairs, fh * pairs
    row, col, core = place()[:3]
    even = lax.rem(col, 2) == 0

    def put(at, first, last):
        out_near[at] = jnp.where(even, last, first)
        out_far[at] = jnp.where(even, first, last)

    for f_at, c_at, is_up in ((0, 0, True), (FH + fh, TH + fh, False)):
        other = core == 0 if is_up else core == 1
        for r in range(FH):
            for p in range(pairs):
                ends = []
                for col_at in (2 * p, fw - FH + 2 * p):
                    here = slice(col_at, col_at + 2)
                    ends.append(jnp.where(other, far[r, here], near[r, here]))
                put((f_at + r) * pairs + p, *ends)
        for r in range(TH * parts):
            ends = []
            for col_at in (0, fw - TH):
                here = slice(col_at, col_at + TH)
                ends.append(jnp.where(other, far[FH + r, here], near[FH + r, here]))
            put(tall + c_at * parts + r, *ends)
    for out, here, there in ((out_near, edge1, edge0), (out_far, edge0, edge1)):
        out[FH * pairs : (FH + fh) * pairs] = jnp.where(even, here[0:thin], there[0:thin])
        out[tall + TH * parts : tall + (TH + fh) * parts] = jnp.where(
            even, here[thin : thin + fh * parts], there[thin : thin + fh * parts]
        )


def forward_kernel(
    fw, fh, feat, r_near, r_far, c_near, c_far, kern, gains, shifts, act, rim, x_ref, acc_ref
):
    slot = fw + TAIL
    count = act.shape[0]
    ch = x_ref.shape[1]
    pairs = FH // 2
    row, col, core, xbit, ybit, chip = place()
    even = lax.rem(col, 2) == 0
    none = jnp.zeros((2, ch), BF)
    for s in range(fh + 2 * FH + 1):
        at = s * slot
        if s == 0:
            piece = jnp.zeros((fw, ch), BF)
        elif s <= FH:
            piece = jnp.where(core == 0, r_far[s - 1], r_near[s - 1])
        elif s <= FH + fh:
            piece = feat[s - 1 - FH]
        else:
            piece = jnp.where(core == 0, r_near[s - 1 - FH - fh], r_far[s - 1 - FH - fh])
        x_ref[at : at + fw] = piece
        tail = []
        for r, first, second in ((s - 1, c_near, c_far), (s, c_far, c_near)):
            for p in range(pairs):
                n = r * pairs + p
                tail.append(jnp.where(even, first[n], second[n]) if 0 <= r < fh + 2 * FH else none)
        x_ref[at + fw : at + slot] = jnp.concatenate(tail, axis=0)
    conv(lambda i: x_ref[i * slot : i * slot + count], kern, acc_ref, count, False)
    pre = gains[0:1] * acc_ref[...] + shifts[0:1]
    out = (jnp.maximum(pre, 0.0) * in_image(1, count, slot, fw, fh)).astype(BF)
    act[...] = out
    acc_ref[...] = out.astype(F32)
    for r, part in rimmed(acc_ref, 3 * slot, slot, fw, fh):
        rim[r] = part


def put_turned(out, value, lanes):
    row, col, core, xbit, ybit, chip = place()
    size = value.shape[0] // 8
    for q in range(4):
        for k in range(2):
            at = (lax.bitwise_xor(core, k) * 4 + lax.bitwise_xor(chip, q)) * size
            block = 2 * q + k
            out[pl.ds(pl.multiple_of(at, size), size), lanes] = value[block * size : (block + 1) * size]


def head_kernel(
    fw, fh, a1, kern, gains, shifts, hw_ref, bias, scale, ct, ct_code, r_near, r_far, c_near, c_far,
    head_out, dy, dy_own, dy_other, turned, dh_ref, gu_ref, hot,
    acc_ref, a2_ref, code_ref, level_ref, out_ref, sems, *others,
):
    slot = fw + TAIL
    h_refs, s_refs, ct_refs = others[0:2], others[2:4], others[4:6]
    count, ch = dy.shape
    ho = ct.shape[2]
    rows = fh + 2 * TH + 1
    lo, hi = (TH + 1) * slot, (TH + 1 + fh) * slot
    row, col, core, xbit, ybit, chip = place()

    parts = -(-(ho + 128) // ch)
    thin = (fh + 2 * FH) * (FH // 2)
    even = lax.rem(col, 2) == 0

    def spread(dst, q, lanes, first):
        wide = dst.shape[1]
        dst[0:fw] = jnp.zeros((fw, wide), BF)
        none = jnp.zeros((TH, wide), BF)
        for s in range(rows):
            if 0 < s <= TH:
                at = FH + (s - 1) * parts + q
                dst[s * slot : s * slot + fw] = jnp.where(
                    core == 0, r_far[at, :, lanes], r_near[at, :, lanes]
                )
            elif TH < s <= TH + fh:
                dst[s * slot : s * slot + fw] = first(s - 1 - TH)
            elif s > 0:
                at = FH + (s - 1 - TH - fh) * parts + q
                dst[s * slot : s * slot + fw] = jnp.where(
                    core == 0, r_near[at, :, lanes], r_far[at, :, lanes]
                )
            right = left = none
            if s > 0:
                at = thin + (s - 1) * parts + q
                right = jnp.where(even, c_near[at, :, lanes], c_far[at, :, lanes])
            if s < rows - 1:
                at = thin + s * parts + q
                left = jnp.where(even, c_far[at, :, lanes], c_near[at, :, lanes])
            tail = [right, jnp.zeros((TAIL - 2 * TH, wide), BF), left]
            dst[s * slot + fw : (s + 1) * slot] = jnp.concatenate(tail, axis=0)

    conv(lambda i: a1[i * slot : i * slot + count], kern, acc_ref, count, False)
    act = jnp.maximum(gains[1:2] * acc_ref[...] + shifts[1:2], 0.0).astype(BF)
    a2_ref[...] = act
    index = lax.broadcasted_iota(jnp.int32, (hi - lo, 1), 0)
    inner = lax.rem(index, slot) < fw
    put_turned(turned, jnp.where(inner, act[lo:hi], jnp.zeros_like(act[lo:hi])).T, slice(None))
    spread(code_ref, ho // ch, pl.ds(ho % ch, 128), lambda r: ct_code[r])
    code = code_ref[...].astype(F32)
    lane = lax.broadcasted_iota(jnp.int32, (count, 128), 1)
    turn = jnp.where(lane < SCALES, lane, jnp.where(lane < 2 * SCALES, lane - SCALES, lane - 2 * SCALES))
    wanted = jnp.where(lane < 3 * SCALES, turn + 1, -1).astype(F32)
    level = jnp.where(code == wanted, 1.0, 0.0)
    level_ref[...] = level.astype(BF)
    core_level = jnp.where(lane[lo:hi] < SCALES, level[lo:hi], jnp.where(lane[lo:hi] == SCALES, 1.0, 0.0))
    hot[...] = jnp.where(inner, core_level, 0.0).astype(BF).T[: hot.shape[0]]

    def product(g):
        lanes = slice(g * HC, (g + 1) * HC)
        h_refs[g % 2][...] = jnp.dot(a2_ref[...], hw_ref[:, lanes], preferred_element_type=F32)

    def leave(g):
        lanes = slice(g * HC, (g + 1) * HC)
        return pltpu.make_async_copy(out_ref.at[g % 2], head_out.at[:, :, lanes], sems.at[g % 2])

    product(0)
    block = count // rows * 3
    for g in range(HEADS):
        lanes = slice(g * HC, (g + 1) * HC)
        h_ref, s_ref, ct_ref = h_refs[g % 2], s_refs[g % 2], ct_refs[g % 2]
        if g + 1 < HEADS:
            product(g + 1)
        inside = slice(g * HC % ch, g * HC % ch + HC)
        spread(ct_ref, g * HC // ch, inside, lambda r, lanes=lanes: ct[r, :, lanes])
        whole = scale[:, lanes]
        terms = []
        for _ in range(3):
            term = whole.astype(BF)
            terms.append(term.astype(F32))
            whole = whole - terms[-1]
        terms.append(jnp.zeros((128 - 3 * SCALES, HC), F32))
        terms = jnp.concatenate(terms, axis=0).astype(BF)
        s_ref[...] = jnp.dot(level_ref[...], terms, preferred_element_type=F32)
        offset = bias[lanes]
        if g >= 2:
            leave(g - 2).wait()
        for at in range(0, count, block):
            here = slice(at, at + block)
            h = h_ref[here] + offset
            inv = lax.rsqrt(jnp.sum(h * h, axis=1, keepdims=True) + EPS)
            u = h * inv
            s = s_ref[here]
            up = ct_ref[here].astype(F32)
            du = up * s
            along = jnp.sum(du * u, axis=1, keepdims=True)
            dh_ref[here, lanes] = (inv * (du - u * along)).astype(BF)
            gu_ref[here, lanes] = (up * u).astype(BF)
            out = (s * u).astype(BF)
            for r in range(at // slot, (at + block) // slot):
                if TH + 1 <= r < TH + 1 + fh:
                    out_ref[g % 2, r - TH - 1] = out[r * slot - at : r * slot - at + fw]
        leave(g).start()
    for g in (HEADS - 2, HEADS - 1):
        leave(g).wait()
    acc_ref[...] = lax.dot_general(
        dh_ref[...], hw_ref[...], (((1,), (1,)), ((), ())), preferred_element_type=F32
    )
    grad = jnp.where(a2_ref[...] > 0.0, gains[1:2] * acc_ref[...], 0.0).astype(BF)
    dy[...] = grad
    for r in range(fh):
        at = lo + r * slot
        put_shares(r, grad[at : at + fw], dy_own, dy_other)


def head_weight_kernel(lo, turned, dh_ref, gu_ref, hot, keep, send, small):
    count = keep.shape[0]
    span = turned.shape[1]
    for g in range(HEADS):
        lanes = slice(g * HC, (g + 1) * HC)
        dh = dh_ref[lo : lo + span, lanes]
        keep[:, lanes] = jnp.dot(turned[0:count], dh, preferred_element_type=F32).astype(BF)
        send[0:count, lanes] = jnp.dot(turned[count:], dh, preferred_element_type=F32).astype(BF)
        scale_part = jnp.dot(hot[...], gu_ref[lo : lo + span, lanes], preferred_element_type=F32)
        bias_part = jnp.dot(hot[...], dh, preferred_element_type=F32)
        pick = lax.broadcasted_iota(jnp.int32, scale_part.shape, 0)
        rest = jnp.where(pick < SCALES, scale_part, bias_part)[:4]
        small[:, lanes] = rest
        high = rest.astype(BF).astype(F32)
        terms = [high, rest - high, jnp.zeros((8, HC), F32)]
        send[count : count + 16, lanes] = jnp.concatenate(terms, axis=0).astype(BF)


def back_kernel(fw, fh, dy2, kern, gains, a1, dy1, own, other, acc_ref):
    slot = fw + TAIL
    count = dy1.shape[0]
    conv(lambda i: dy2[i * slot : i * slot + count], kern, acc_ref, count, True)
    grad = jnp.where(
        a1[2 * slot : 2 * slot + count] > 0.0, gains[0:1] * acc_ref[...], 0.0
    ).astype(BF)
    dy1[...] = grad
    acc_ref[...] = grad.astype(F32)
    for r, part in rimmed(acc_ref, slot, slot, fw, fh):
        put_shares(r, part, own, other)


def input_kernel(fw, fh, dy1, kern, out, acc_ref):
    slot = fw + TAIL
    lead = slot // 2
    count = fh * slot + lead
    conv(
        lambda i: dy1[(i + 1) * slot - lead : (i + 1) * slot - lead + count],
        kern, acc_ref, count, True,
    )
    for r in range(fh):
        out[r] = acc_ref[lead + r * slot : lead + r * slot + fw]


def weight_kernel(fw, fh, forward, flat0, flat1, wide0, wide1, keep, send, turn_ref, wide_ref, shift_ref, part_ref):
    slot = fw + TAIL
    core, chip = place()[2], place()[5]
    full = fh * slot
    length, lanes = wide_ref.shape
    lead = slot // 2
    for b, (flat, wide) in enumerate(((flat0, wide0), (flat1, wide1))):
        rows = []
        gap = jnp.zeros((TAIL, flat.shape[2]), BF)
        for r in range(fh):
            rows += [flat[r], gap]
        turned = jnp.concatenate(rows, axis=0).T
        if forward:
            turn_ref[:, b * full : (b + 1) * full] = turned
        else:
            put_turned(turn_ref, turned, slice(b * full, (b + 1) * full))
        wide_ref[0:lead] = jnp.zeros((lead, lanes), F32)
        for r in range(fh + 2):
            at = lead + r * slot
            wide_ref[at : at + fw] = wide[r].astype(F32)
            wide_ref[at + fw : at + slot] = jnp.zeros((TAIL, lanes), F32)
        for k, at in ((fh + 2, lead - 1), (fh + 3, lead + fw)):
            column = wide[k].astype(F32)
            for t in range(fh + 2):
                wide_ref[at + t * slot : at + t * slot + 1] = column[t : t + 1]
        value = wide_ref[...]
        shift_ref[0, b] = pltpu.roll(value, 1, 0).astype(BF)
        shift_ref[1, b] = value.astype(BF)
        shift_ref[2, b] = pltpu.roll(value, length - 1, 0).astype(BF)
    base = lead + slot
    size = keep.shape[2]
    for i in range(3):
        for j in range(3):
            row, col = (i, j) if forward else (2 - i, 2 - j)
            at = base + (row - 1) * slot
            total = None
            for b in range(2):
                term = jnp.dot(
                    turn_ref[:, b * full : (b + 1) * full],
                    shift_ref[col, b, at : at + full],
                    preferred_element_type=F32,
                )
                total = term if total is None else total + term
            tap = 3 * i + j
            if forward:
                part_ref[...] = total.T
                for m in range(4):
                    block = 2 * lax.bitwise_xor(chip, m)
                    mine = pl.multiple_of((block + core) * size, size)
                    theirs = pl.multiple_of((block + 1 - core) * size, size)
                    keep[m, tap] = part_ref[pl.ds(mine, size), :].astype(BF)
                    send[m, tap] = part_ref[pl.ds(theirs, size), :].astype(BF)
                continue
            total = total.astype(BF)
            for m in range(4):
                keep[m, tap] = total[m * size : (m + 1) * size]
                send[m, tap] = total[(4 + m) * size : (5 + m) * size]


def pair_kernel(order, got, keep, own, send):
    for n, m in enumerate(order):
        total = keep[m].astype(F32) + got[m].astype(F32)
        if n < 2:
            own[n] = total
        else:
            send[n - 2] = total.astype(BF)


def line_kernel(got, own, out, send):
    out[...] = own[0] + got[0].astype(F32)
    send[...] = (own[1] + got[1].astype(F32)).astype(BF)


def plane_kernel(got, own, out, send):
    part = out.shape[2]
    high = (place()[1] >> 1) & 1
    for tap in range(own.shape[0]):
        total = own[tap] + got[tap].astype(F32)
        left, right = total[:, :part], total[:, part:]
        out[tap] = jnp.where(high == 0, left, right)
        send[tap] = jnp.where(high == 0, right, left).astype(BF)


def final_kernel(got1, own1, got2, own2, out):
    out[0] = own1[...] + got1[...].astype(F32)
    out[1] = own2[...] + got2[...].astype(F32)


def put_rest(send, at, small):
    lanes = send.shape[1]
    high = small.astype(BF).astype(F32)
    rows = []
    for n in range(small.shape[1] // lanes):
        here = slice(n * lanes, (n + 1) * lanes)
        rows += [high[:, here], (small - high)[:, here]]
    if len(rows) % 4:
        rows += [jnp.zeros_like(rows[0])] * 2
    for n in range(0, len(rows), 4):
        send[at + 4 * n : at + 4 * n + 16] = jnp.concatenate(rows[n : n + 4], axis=0).astype(BF)


def get_rest(got, at, rest, out):
    lanes = got.shape[1]
    for n in range(rest.shape[1] // lanes):
        here = slice(n * lanes, (n + 1) * lanes)
        terms = got[at + 16 * (n // 2) : at + 16 * (n // 2) + 16].astype(F32)
        first = 8 * (n % 2)
        out[:, here] = rest[:, here] + terms[first : first + 4] + terms[first + 4 : first + 8]


def head_pair_kernel(got, keep, small, own, rest, send):
    size, wide = own.shape
    part = wide // 2
    low = place()[1] & 1
    total = keep[...].astype(F32) + got[0:size].astype(F32)
    chunks = [total[:, c * part : (c + 1) * part] for c in range(4)]
    for m in range(2):
        even, odd = chunks[2 * m], chunks[2 * m + 1]
        lanes = slice(m * part, (m + 1) * part)
        own[:, lanes] = jnp.where(low == 0, even, odd)
        send[0:size, lanes] = jnp.where(low == 0, odd, even).astype(BF)
    get_rest(got, size, small, rest)
    put_rest(send, size, rest[...])


def head_join_kernel(got, own, rest, own_out, rest_new, send):
    size = own_out.shape[0]
    own_out[...] = own[0:size] + got[0:size].astype(F32)
    send[0:size] = (own[size:] + got[size : 2 * size].astype(F32)).astype(BF)
    get_rest(got, 2 * size, rest, rest_new)
    put_rest(send, size, rest_new[...])


def head_quarter_kernel(got, own, rest, own_out, rest_new, send):
    size, part = own_out.shape
    low = (place()[1] >> 1) & 1
    total = own[...] + got[0:size].astype(F32)
    left, right = total[:, :part], total[:, part:]
    own_out[...] = jnp.where(low == 0, left, right)
    send[0:size] = jnp.where(low == 0, right, left).astype(BF)
    get_rest(got, size, rest, rest_new)
    put_rest(send, size, rest_new[...])


def head_last_kernel(got, own, rest, out, scale, bias, total):
    size, part = own.shape
    out[...] = own[...] + got[0:size].astype(F32)
    get_rest(got, size, rest, total)
    scale[...] = total[0:SCALES]
    bias[...] = total[SCALES]


def after(value, done):
    return lax.optimization_barrier((value, done))


def paired(near, far, axis):
    peers = lax.axis_size(axis)
    first = [(i, i ^ 1) for i in range(peers)]
    second = [(i, ((i + 1) ^ 1) - 1) for i in range(1, peers - 1)]
    return lax.ppermute(near, axis, first), lax.ppermute(far, axis, second)


def crossed(array, bits):
    peers = lax.axis_size("rows")
    return lax.ppermute(array, "rows", [(i, i ^ bits) for i in range(peers)])


def across(array, bits):
    peers = lax.axis_size("cols")
    return lax.ppermute(array, "cols", [(i, i ^ bits) for i in range(peers)])


def call(kernel, name, outs, args, scratch=(), far=0, leave=0):
    near = len(args) - far
    spaces = [pltpu.VMEM] * near + [pltpu.HBM] * far
    args = [pltpu.with_memory_space_constraint(a, s) for a, s in zip(args, spaces)]
    return pl.pallas_call(
        kernel,
        out_shape=tuple(pltpu.VMEM(*out) if isinstance(out, tuple) else out for out in outs),
        in_specs=[VMEM] * near + [HBM] * far,
        out_specs=(HBM,) * leave + (VMEM,) * (len(outs) - leave),
        scratch_shapes=[pltpu.VMEM(*s) if isinstance(s, tuple) else s for s in scratch],
        compiler_params=pltpu.CompilerParams(vmem_limit_bytes=24 * 1024 * 1024),
        cost_estimate=pl.CostEstimate(flops=COSTS.get(name, 10**10), bytes_accessed=0, transcendentals=0),
        name=name,
    )(*args)


def shards(
    features, kernels, gains, shifts, head_weight, head_bias, head_scale, scale_id, valid, cotangent
):
    rows, cols = lax.axis_size("rows"), lax.axis_size("cols")
    feat, ct = features[0], cotangent[0]
    fh, fw, ch = feat.shape
    ho = ct.shape[2]
    slot = fw + TAIL
    span = fh * slot
    shape = jax.ShapeDtypeStruct
    half = ch // 2
    size = ch // 8
    part = ho // 4
    fast = rows == 8 and cols == 4

    parts = -(-(ho + 128) // ch)
    message = ((FH + TH * parts, fw, ch), BF)
    edge = ((fh * (FH // 2 + parts), 2, ch), BF)
    feat, ct, code, near, far, edge0, edge1 = call(
        functools.partial(prepare_kernel, fw, fh),
        "prepare",
        (((fh, fw, ch), BF), ((fh, fw, ho), BF), ((fh, fw, 128), BF), message, message, edge, edge),
        (feat, ct, scale_id, valid),
        [pltpu.VMEM(scale_id.shape, jnp.int32), pltpu.VMEM(valid.shape, jnp.int32), DMA((4,))],
        far=4,
    )

    def load(layer, extra, done):
        args, done = after((kernels.reshape(2, 9, ch, ch), *extra), done)
        outs = [((9, ch, ch), BF)] + [(a.shape, BF) for a in extra]
        loaded = call(
            functools.partial(load_kernel, layer), f"load{layer}", outs, args, [DMA((2,))], far=len(args)
        )
        return loaded, done

    by_row = paired(near, far, "rows")
    (taps1,), edge0 = load(0, (), edge0)
    (taps2, head_weight), taps1 = load(1, (head_weight,), taps1)
    edge0, taps2 = after(edge0, taps2)
    edge = (((fh + 2 * FH) * (FH // 2) + (fh + 2 * TH) * parts, 2, ch), BF)
    near, far = call(
        functools.partial(lengthen_kernel, fh), "lengthen", (edge, edge), (edge0, edge1, *by_row)
    )
    by_col = paired(near, far, "cols")
    feat, near = after(feat, near)

    core = ((fh, fw, half), BF)
    n1 = (fh + 2 * FH - 1) * slot
    a1, a1_rim = call(
        functools.partial(forward_kernel, fw, fh),
        "conv1",
        (((n1, ch), BF), ((fh + 4, fw, ch), BF)),
        (feat, *by_row, *by_col, taps1, gains, shifts),
        [((n1 + 2 * slot, ch), BF), ((n1, ch), F32)],
    )

    n2 = (fh + 2 * TH + 1) * slot
    lo = (TH + 1) * slot
    head_out, dy2, dy2_own, dy2_other, turned, dh, gu, hot = call(
        functools.partial(head_kernel, fw, fh),
        "head",
        (shape((fh, fw, ho), BF), ((n2, ch), BF), core, core, ((ch, span), BF))
        + (((n2, ho), BF), ((n2, ho), BF), ((16, span), BF)),
        (a1, taps2, gains, shifts, head_weight, head_bias, head_scale, ct, code, *by_row, *by_col),
        [((n2, ch), F32), ((n2, ch), BF), ((n2, 128), BF), ((n2, 128), BF)]
        + [((2, fh, fw, HC), BF), DMA((2,))]
        + [((n2, HC), F32)] * 4
        + [((n2, HC), BF)] * 2,
        leave=1,
    )
    n3 = (fh + 3) * slot
    rim = ((fh + 4, fw, half), BF)
    rest = ((4, ho), F32)
    block = (9, size, half)
    blocks = (2,) + block
    chunk = (9, size, half // 2)
    halves = ((blocks, F32), (blocks, BF))
    lines = ((block, F32), (block, BF))
    chunks = ((chunk, F32), (chunk, BF))
    parted = ((4, 9, size, half), BF)
    length = (fh + 2) * slot + slot // 2

    def grad_scratch(flat, wide):
        return [((flat, 2 * span), BF), ((length, wide), F32), ((3, 2, length, wide), BF), ((ch, half), F32)]

    kernel = functools.partial
    tasks = {
        "headweight": (
            kernel(head_weight_kernel, lo),
            (((4 * size, ho), BF), ((4 * size + 16, ho), BF), rest),
            (),
            (turned, dh, gu, hot),
            "hw_keep hw_send small0",
        ),
        "back2": (
            kernel(back_kernel, fw, fh),
            (((n3, ch), BF), rim, rim),
            [((n3, ch), F32)],
            (dy2, taps2, gains, a1),
            "dy1 dy1_own dy1_other",
        ),
        "back1": (
            kernel(input_kernel, fw, fh),
            (shape((fh, fw, ch), F32),),
            [((span + slot // 2, ch), F32)],
            ("dy1", taps1),
            "grad_features",
        ),
        "grad2": (
            kernel(weight_kernel, fw, fh, True),
            (parted, parted),
            grad_scratch(half, ch),
            ("dy2_in", dy2_own, "a1_in", a1_rim),
            "keep2 send2",
        ),
        "grad1": (
            kernel(weight_kernel, fw, fh, False),
            (parted, parted),
            grad_scratch(ch, half),
            ("a0_in", feat, "dy1_in", "dy1_own"),
            "keep1 send1",
        ),
        "pair2": (kernel(pair_kernel, (0, 2, 1, 3)), halves, (), ("pair2_in", "keep2"), "own2 x2"),
        "pair1": (kernel(pair_kernel, (0, 1, 2, 3)), halves, (), ("pair1_in", "keep1"), "own1 y1"),
        "line2": (line_kernel, lines, (), ("x2_in", "own2"), "part2 y2"),
        "line1": (line_kernel, lines, (), ("y1_in", "own1"), "part1 x1"),
        "plane2": (plane_kernel, chunks, (), ("y2_in", "part2"), "own2z z2"),
        "plane1": (plane_kernel, chunks, (), ("x1_in", "part1"), "own1z z1"),
        "final": (
            final_kernel,
            (shape((2,) + chunk, F32),),
            (),
            ("z1_in", "own1z", "z2_in", "own2z"),
            "grad_kernels",
        ),
        "headpair": (
            head_pair_kernel,
            (((4 * size, 2 * part), F32), rest, ((4 * size + 16, 2 * part), BF)),
            (),
            ("hw_in", "hw_keep", "small0"),
            "hw1 small1 hw_z1",
        ),
        "headline": (
            head_join_kernel,
            (((2 * size, 2 * part), F32), rest, ((2 * size + 16, 2 * part), BF)),
            (),
            ("hw_z1_in", "hw1", "small1"),
            "hw2 small2 hw_y",
        ),
        "headplane": (
            head_join_kernel,
            (((size, 2 * part), F32), rest, ((size + 16, 2 * part), BF)),
            (),
            ("hw_y_in", "hw2", "small2"),
            "hw3 small3 hw_x",
        ),
        "headmiddle": (
            head_quarter_kernel,
            (((size, part), F32), rest, ((size + 32, part), BF)),
            (),
            ("hw_x_in", "hw3", "small3"),
            "hw4 small4 hw_z2",
        ),
        "headlast": (
            head_last_kernel,
            (shape((size, part), F32), shape((SCALES, ho), F32), shape((ho,), F32)),
            [((4, ho), F32)],
            ("hw_z2_in", "hw4", "small4"),
            "grad_head_weight grad_head_scale grad_head_bias",
        ),
    }
    sent = {
        "a0_in": (feat, across, 1),
        "a1_in": (a1_rim, across, 1),
        "dy2_in": (dy2_other, across, 1),
        "dy1_in": ("dy1_other", across, 1),
        "pair2_in": ("send2", crossed, 1),
        "pair1_in": ("send1", crossed, 1),
        "x2_in": ("x2", crossed, 2),
        "y2_in": ("y2", crossed, 4),
        "z2_in": ("z2", across, 2),
        "y1_in": ("y1", crossed, 4),
        "x1_in": ("x1", crossed, 2),
        "z1_in": ("z1", across, 2),
        "hw_in": ("hw_send", crossed, 1),
        "hw_y_in": ("hw_y", crossed, 4),
        "hw_x_in": ("hw_x", crossed, 2),
        "hw_z1_in": ("hw_z1", across, 1),
        "hw_z2_in": ("hw_z2", across, 2),
    }
    known = {}

    def value(name):
        if not isinstance(name, str):
            return name
        if name not in known:
            what, exchange, bits = sent[name]
            known[name] = exchange(value(what), bits)
        return known[name]

    if fast:
        done = dy2
        for name in ORDER:
            body, outs, scratch, names, results = tasks[name]
            args = [value(n) for n in names]
            early = [value(n) for n in EARLY.get(name, ())]
            (args[0], *early), done = after((args[0], *early), done)
            for n, a in zip(EARLY.get(name, ()), early):
                known[n] = a
            made = call(body, name, outs, args, scratch)
            known.update(zip(results.split(), made))
            done = made[0]
        grad_features = known["grad_features"]
        grad_kernels = known["grad_kernels"].reshape(2, 3, 3, size, half // 2)
        grad_head_weight, grad_head_scale = known["grad_head_weight"], known["grad_head_scale"]
        grad_head_bias = known["grad_head_bias"]
    else:
        row = lax.axis_index("rows")
        for name in ("headweight", "back2", "back1"):
            body, outs, scratch, names, results = tasks[name]
            made = call(body, name, outs, [value(n) for n in names], scratch)
            known.update(zip(results.split(), made))
        grad_features, dy1, small = known["grad_features"], known["dy1"], known["small0"]
        hw_keep, hw_send = known["hw_keep"], known["hw_send"]
        flat = jnp.pad(feat, ((0, 0), (0, TAIL), (0, 0))).reshape(span, ch)
        dy2_flat = dy2[(TH + 1) * slot :][:span].reshape(fh, slot, ch)[:, :fw]
        dy2_flat = jnp.pad(dy2_flat, ((0, 0), (0, TAIL), (0, 0))).reshape(span, ch)
        parts = []
        for left, right, first, sign in ((flat, jnp.pad(dy1, ((0, 8), (0, 0))), 2, -1), (a1, dy2_flat, 4, 1)):
            for i in (-1, 0, 1):
                for j in (-1, 0, 1):
                    at = (first + sign * i) * slot + sign * j
                    if sign < 0:
                        pair = (left, right[at : at + span])
                    else:
                        pair = (left[at : at + span], right)
                    parts.append(jnp.einsum("pc,pk->ck", *pair, preferred_element_type=F32).astype(BF))
        total = jnp.stack(parts).reshape(2, 3, 3, ch, ch)
        total = lax.psum_scatter(total, "cols", scatter_dimension=4, tiled=True)
        grad_kernels = lax.psum_scatter(
            total.astype(F32), "rows", scatter_dimension=3, tiled=True
        )
        at = (row >> 1) & 3
        order = [(at ^ m) * 2 for m in range(4)]
        hw_keep, hw_send = hw_keep.reshape(4, size, ho), hw_send[: 4 * size].reshape(4, size, ho)
        blocks = jnp.zeros((8, size, ho), BF)
        for m in range(4):
            blocks = lax.dynamic_update_slice(blocks, hw_keep[m : m + 1], (order[m] + (row & 1), 0, 0))
            blocks = lax.dynamic_update_slice(blocks, hw_send[m : m + 1], (order[m] + 1 - (row & 1), 0, 0))
        part = lax.psum_scatter(blocks.reshape(ch, ho), "cols", scatter_dimension=1, tiled=True)
        grad_head_weight = lax.psum_scatter(part.astype(F32), "rows", scatter_dimension=0, tiled=True)
        small = lax.psum(small[:4], ("rows", "cols"))
        grad_head_scale, grad_head_bias = small[:SCALES], small[SCALES]
    return (
        head_out[None],
        grad_features[None],
        grad_kernels,
        grad_head_weight,
        grad_head_bias,
        grad_head_scale,
    )


def solution(mesh):
    return jax.shard_map(
        shards,
        mesh=mesh,
        in_specs=(
            P(None, "rows", "cols", None),
            P(),
            P(),
            P(),
            P(),
            P(),
            P(),
            P(None, "rows", "cols"),
            P(None, "rows", "cols"),
            P(None, "rows", "cols", None),
        ),
        out_specs=(
            P(None, "rows", "cols", None),
            P(None, "rows", "cols", None),
            P(None, None, None, "rows", "cols"),
            P("rows", "cols"),
            P(),
            P(),
        ),
        check_vma=False,
    )
```
